512 devices in a mesh: leaf: 8 (over x, core), sub: 64 (over z, y).
Axes of the slice: x: 4, y: 8, z: 8, core: 2. Of those that a mesh axis runs over, the one named last changes fastest.
Arguments:
- points: bfloat16 [131072, 64], P(('leaf', 'sub')), may hold values from -6 to 6
- omega: bfloat16 [131072, 256], P(('leaf', 'sub')), may hold values from -6 to 6
- samples: float32 [131072, 256], P(('leaf', 'sub')), may hold values from -48 to 48
- ranks: int32 [8, 4], P('leaf'), may hold values from 128 to 256, as said below
- leaf_skeleton: int32 [8, 256], P('leaf'), may hold values from 0 to 16383, as said below
- merge_skeleton: int32 [8, 3, 256], P('leaf'), may hold values from 0 to 511, as said below
Outputs:
- leaf_interp: float32 [131072, 256], P(('leaf', 'sub'))
- node_interp: float32 [8, 3, 512, 256], P('leaf')
- couplings: float32 [8, 3, 256, 256], P('leaf')
- top_compressed: float32 [8, 256, 256], P('leaf')
The draws below stay inside these ranges and needn't reach their ends.
Inputs may be any that keep to these rules, and one draw needn't show every extreme that they name: ranks[i, l] is the rank of the level-l node holding leaf i (leaves with equal i >> l share it); 256 is reached. `leaf_skeleton`: row i lists 256 distinct point indices within leaf i; the first ranks[i, 0] are its skeleton. merge_skeleton[i, l - 1] lists 256 distinct candidate rows of the level-l node holding leaf i, equal for all its leaves; candidate j < 256 is the lower child's row j, else the upper child's row j - 256; the first ranks[i, l] name rows below the owning child's rank.
All inputs are finite; a program needn't handle non-finite values.
Results may differ from the reference program's by a relative error of at most 0.00076.
Values may be sent and summed in bfloat16 or wider, within the bound.
A program may use at most 128 MiB of HBM per device.

```python
import jax
import jax.numpy as jnp
from jax import lax

DIM = 64
S = 256
R = 256
LEVELS = 3
LEAF_PTS = 16384
NPTS = 131072
N_LEAF = 8


def node_ranks(key):
    rank_rows = []
    for height in range(LEVELS + 1):
        count = N_LEAF // 2 ** height
        drawn = jax.random.randint(jax.random.fold_in(key, 100 + height), (count,), R // 2, R + 1).astype(jnp.int32)
        drawn = drawn.at[0].set(R)
        if count > 1:
            drawn = drawn.at[1].set(R // 2)
        rank_rows.append(drawn)
    return rank_rows


def draw_ranks(key, part):
    rank_rows = node_ranks(key)
    leaves = jnp.arange(N_LEAF, dtype=jnp.int32)
    columns = [rank_rows[height][leaves // 2 ** height] for height in range(LEVELS + 1)]
    return jnp.stack(columns, axis=1).astype(jnp.int32)


def draw_leaf_skeleton(key, part):
    leaf_keys = jax.random.split(jax.random.fold_in(key, 7), N_LEAF)
    picker = jax.vmap(lambda single: jax.random.permutation(single, LEAF_PTS)[:R])
    return picker(leaf_keys).astype(jnp.int32)


def merge_pick(single, rank_low, rank_high):
    order = jax.random.permutation(single, 2 * R).astype(jnp.int32)
    slots = jnp.arange(2 * R, dtype=jnp.int32)
    usable = jnp.where(slots < R, slots < rank_low, slots - R < rank_high)
    scores = jnp.where(usable, 0, 2 * R).astype(jnp.int32) + order
    return jnp.argsort(scores, stable=True)[:R].astype(jnp.int32)


def draw_merge_skeleton(key, part):
    rank_rows = node_ranks(key)
    leaves = jnp.arange(N_LEAF, dtype=jnp.int32)
    tables = []
    for height in range(1, LEVELS + 1):
        count = N_LEAF // 2 ** height
        node_keys = jax.random.split(jax.random.fold_in(key, 200 + height), count)
        below = rank_rows[height - 1]
        picked = jax.vmap(merge_pick)(node_keys, below[0::2], below[1::2])
        tables.append(picked[leaves // 2 ** height])
    return jnp.stack(tables, axis=1).astype(jnp.int32)


def block_scale(rng, shape, shards, least, top_value):
    def one(axis_at, blocks):
        draws = jax.random.uniform(jax.random.fold_in(jax.random.fold_in(rng, 6), axis_at), (blocks,), jnp.float32, least / len(shards), top_value / len(shards))
        return jnp.repeat(jnp.exp(draws), shape[axis_at] // blocks).reshape((-1,) + (1,) * (len(shape) - axis_at - 1))

    gain = one(*shards[0])
    for cut in shards[1:]:
        gain = gain * one(*cut)
    return gain


def gaussian(key, extent, spread, bound, cuts=(), kind=jnp.bfloat16):
    values = jax.random.normal(key, extent, jnp.float32) * spread
    if len(cuts) > 0:
        values = block_scale(key, extent, cuts, -0.22, 0.18) * values
    return jnp.clip(values, min=-bound, max=bound).astype(kind)


def setup_inputs(seed: int = 0) -> dict:
    key_list = jax.random.split(jax.random.key(seed), 7)
    points = gaussian(key_list[0], (NPTS, DIM), 1.0, 6.0, ((0, 512),))
    omega = gaussian(key_list[1], (NPTS, S), 1.0, 6.0, ((0, 512),))
    samples = gaussian(key_list[2], (NPTS, S), 8.0, 48.0, ((0, 512),), jnp.float32)
    ranks = draw_ranks(jax.random.fold_in(key_list[6], 71), 0)
    leaf_skeleton = draw_leaf_skeleton(jax.random.fold_in(key_list[6], 71), 0)
    merge_skeleton = draw_merge_skeleton(jax.random.fold_in(key_list[6], 71), 0)
    return {"points": points, "omega": omega, "samples": samples, "ranks": ranks, "leaf_skeleton": leaf_skeleton, "merge_skeleton": merge_skeleton}


def kernel(left, right):
    cross = jnp.einsum('id,jd->ij', left.astype(jnp.float32), right.astype(jnp.float32), precision=lax.Precision.HIGHEST)
    left_sq = jnp.sum(jnp.square(left.astype(jnp.float32)), axis=1)
    right_sq = jnp.sum(jnp.square(right.astype(jnp.float32)), axis=1)
    return jnp.exp(-(left_sq[:, None] + right_sq[None, :] - 2.0 * cross) / (0.5 * left.shape[1]))

def factorize(picked):
    gram = jnp.dot(picked.astype(jnp.float32), picked.T.astype(jnp.float32), precision=lax.Precision.HIGHEST, preferred_element_type=jnp.float32)
    shift = jnp.sum(picked * picked) / picked.shape[0] + 1e-06
    return jnp.linalg.cholesky(gram + shift * jnp.eye(picked.shape[0], dtype=jnp.float32))

def interpolate(factor, candid, picked):
    right_side = jnp.einsum('rs,ns->rn', picked, candid, precision=lax.Precision.HIGHEST)
    return jax.scipy.linalg.cho_solve((factor, True), right_side).T

def leaf_node(inputs):
    node_pts, node_omega, node_samples, skeleton, rank_now = inputs
    weights = kernel(node_pts, node_pts).astype(jnp.bfloat16)
    diag = jnp.dot(weights.astype(jnp.float32), node_omega.astype(jnp.float32), preferred_element_type=jnp.float32)
    resid = node_samples - diag
    live = (jnp.arange(R) < rank_now).astype(jnp.float32)
    picked = resid[skeleton] * live[:, None]
    chosen = node_pts[skeleton].astype(jnp.float32) * live[:, None]
    factor = factorize(picked)
    interp = interpolate(factor, resid, picked)
    compressed = jnp.einsum('nr,ns->rs', interp, node_omega.astype(jnp.float32), precision=lax.Precision.HIGHEST)
    return (interp, chosen, picked, compressed, live)

def merge_node(inputs):
    x_low, x_high, y_low, y_high, o_low, o_high, m_low, m_high, skeleton, rank_now = inputs
    coupling = m_low[:, None] * m_high[None, :] * kernel(x_low.astype(jnp.bfloat16), x_high.astype(jnp.bfloat16))
    new_low = y_low - jnp.dot(coupling, o_high, precision=lax.Precision.HIGHEST)
    new_high = y_high - jnp.einsum('ij,is->js', coupling, o_low, precision=lax.Precision.HIGHEST)
    cand_y = jnp.concatenate([new_low, new_high], axis=0)
    cand_x = jnp.concatenate([x_low, x_high], axis=0)
    cand_o = jnp.concatenate([o_low, o_high], axis=0)
    live = (jnp.arange(R) < rank_now).astype(jnp.float32)
    picked = cand_y[skeleton] * live[:, None]
    chosen = cand_x[skeleton] * live[:, None]
    factor = factorize(picked)
    interp = interpolate(factor, cand_y, picked)
    compressed = jnp.einsum('nr,ns->rs', interp, cand_o, precision=lax.Precision.HIGHEST)
    return (coupling, interp, chosen, picked, compressed, live)

def reference(points, omega, samples, ranks, leaf_skeleton, merge_skeleton):
    node_pts = points.reshape(N_LEAF, LEAF_PTS, DIM)
    node_omega = omega.reshape(N_LEAF, LEAF_PTS, S)
    node_samples = samples.reshape(N_LEAF, LEAF_PTS, S)
    interp, chosen, picked, compressed, live = lax.map(leaf_node, (node_pts, node_omega, node_samples, leaf_skeleton, ranks[:, 0]))
    leaf_interp = interp.reshape(N_LEAF * LEAF_PTS, R)
    interp_levels = []
    couple_levels = []
    for height in range(1, LEVELS + 1):
        stride = 2 ** height
        skeleton = merge_skeleton[::stride, height - 1]
        rank_now = ranks[::stride, height]
        coupling, interp, chosen, picked, compressed, live = lax.map(merge_node, (chosen[0::2], chosen[1::2], picked[0::2], picked[1::2], compressed[0::2], compressed[1::2], live[0::2], live[1::2], skeleton, rank_now))
        interp_levels.append(jnp.repeat(interp, stride, axis=0))
        paired = jnp.stack([coupling, jnp.swapaxes(coupling, 1, 2)], axis=1).reshape(-1, R, R)
        couple_levels.append(jnp.repeat(paired, stride // 2, axis=0))
    node_interp = jnp.stack(interp_levels, axis=1)
    couplings = jnp.stack(couple_levels, axis=1)
    top_compressed = jnp.repeat(compressed, 2 ** LEVELS, axis=0)
    return (leaf_interp, node_interp, couplings, top_compressed)
```

```python
import jax
import jax.numpy as jnp
from jax import lax
from jax.experimental import pallas as pl
from jax.experimental.pallas import tpu as pltpu
from jax.sharding import PartitionSpec as P

F32 = jnp.float32
BF16 = jnp.bfloat16
RING = 8
N = 256
AUG = 128
CUT = N // RING
LEVELS = 3
OWN = RING // 2 - 1
NN = ((1,), (0,))
NT = ((1,), (1,))
TN = ((0,), (0,))
DEAD = -1e30
MESH = pl.DeviceIdType.MESH

SPAN = N + 1.0
SIGMA = (SPAN + 1.0) / (SPAN - 1.0)
CHEB = 2.0 * SIGMA * SIGMA - 1.0
ALPHA = 8.0 * (SPAN + 1.0) / ((SPAN - 1.0) ** 2 * CHEB)
BETA = 8.0 / ((SPAN - 1.0) ** 2 * CHEB)
RATES = []
RHO = 1.0 / CHEB
for _ in range(6):
    RATES.append(2.0 / (2.0 - RHO * RHO))
    RHO = RHO * RHO / (2.0 - RHO * RHO)


def bdot(a, b, dims=NN):
    return lax.dot_general(a, b, (dims, ((), ())), preferred_element_type=F32)


def split2(x):
    hi = x.astype(BF16)
    return hi, (x - hi.astype(F32)).astype(BF16)


def split3(x):
    hi = x.astype(BF16)
    rest = x - hi.astype(F32)
    mid = rest.astype(BF16)
    return hi, mid, (rest - mid.astype(F32)).astype(BF16)


def dot3(a, b, dims=NN):
    ah, al = split2(a)
    bh, bl = split2(b)
    return bdot(ah, bh, dims) + (bdot(ah, bl, dims) + bdot(al, bh, dims))


def pick(onehot, x, dims=NN):
    hi, mid, lo = split3(x)
    return bdot(onehot, hi, dims) + bdot(onehot, mid, dims) + bdot(onehot, lo, dims)


def dot6(a, b, dims=NN):
    return lax.dot_general(
        a, b, (dims, ((), ())), precision=lax.Precision.HIGHEST, preferred_element_type=F32
    )


def iota(shape, dim):
    return lax.broadcasted_iota(jnp.int32, shape, dim)


def ridge_inverse(p):
    gram = dot6(p, p, NT)
    inv_shift = 1.0 / (jnp.sum(p * p) / N + 1e-06)
    eye = (iota((N, N), 0) == iota((N, N), 1)).astype(F32)
    b = gram * inv_shift + eye
    x = ALPHA * eye - BETA * b
    e = eye - dot3(b, x)
    for w in RATES:
        eh, el = split2(e)
        xh, xl = split2(x)
        e2 = bdot(eh, eh) + (bdot(eh, el) + bdot(el, eh))
        x = w * (x + (bdot(xh, eh) + (bdot(xh, el) + bdot(xl, eh))))
        e = (1.0 - w) * eye + w * e2
    x = x + dot6(x, eye - dot6(b, x))
    return x * inv_shift


def gauss(left_f, right_g):
    return jnp.exp(bdot(left_f, right_g, NT) * 0.0625)


def body(
    omega_ref, points_ref, samples_ref, skel_ref, mskel_ref, ranks_ref,
    leaf_out, node_out, coup_out, top_out,
    zbuf, ybuf, tot, rsb, base,
    csp, crz, csum, cry, cz, och, xch,
    psp, prz, psum, pry, opk, xpk,
    mtp, mr1, ms1, mr2, mfull, ocm, xcm, onehots, cy, co,
    send_sem, recv_sem,
):
    sub = lax.axis_index("sub")
    leaf = lax.axis_index("leaf")
    z = sub // RING
    y = sub % RING

    def zpeer(d):
        return {"sub": lax.rem(z + d + RING, RING) * RING + y}

    def ypeer(d):
        return {"sub": z * RING + lax.rem(y + d + RING, RING)}

    barrier = pltpu.get_barrier_semaphore()
    for d in range(1, RING):
        pl.semaphore_signal(barrier, inc=1, device_id=zpeer(d), device_id_type=MESH)
        pl.semaphore_signal(barrier, inc=1, device_id=ypeer(d), device_id_type=MESH)
    partners = []
    for level in range(LEVELS):
        bit = (leaf // 2**level) % 2
        partners.append({"leaf": leaf + (1 - 2 * bit) * 2**level})
        pl.semaphore_signal(barrier, inc=1, device_id=partners[-1], device_id_type=MESH)

    copies = []

    def send(src, dst, device):
        at = len(copies)
        copy = pltpu.make_async_remote_copy(
            src_ref=src, dst_ref=dst, send_sem=send_sem.at[at], recv_sem=recv_sem.at[at],
            device_id=device, device_id_type=MESH,
        )
        copy.start()
        copies.append(copy)
        return copy

    def arrive(group):
        for copy in group:
            copy.wait_recv()

    base[...] = jnp.zeros((N, AUG), F32)
    pts = points_ref[...].astype(F32)
    base[:, :64] = pts
    half = -0.5 * jnp.sum(pts * pts, axis=1, keepdims=True)
    h1, h2, h3 = (piece.astype(F32) for piece in split3(half))
    lane = iota((N, AUG), 1)
    plain = base[...]

    def place(at, other):
        out = jnp.where((lane >= other) & (lane < other + 3), 1.0, plain)
        for i, piece in enumerate((h1, h2, h3)):
            out = jnp.where(lane == at + i, piece, out)
        return out.astype(BF16)

    feat = place(64, 67)
    omega = omega_ref[...]
    samples = samples_ref[...]
    eye = (iota((N, N), 0) == iota((N, N), 1)).astype(BF16)
    omega_t = bdot(eye, omega, NT).astype(BF16)
    zbuf[OWN, :, :N] = omega
    zbuf[OWN, :, N:] = place(67, 64)
    ybuf[OWN, :, :N] = omega_t
    ybuf[OWN, :, N:] = feat
    column = iota((1, N), 1)
    offset = skel_ref[...] - sub * N
    hits = (iota((N, N), 0) == offset) & (column < ranks_ref[0, 0])
    hits = hits.astype(F32).astype(BF16)
    hot = bdot(eye, hits, NT).astype(BF16)
    csp[...] = bdot(hot, feat).astype(BF16)

    pl.semaphore_wait(barrier, 2 * (RING - 1) + LEVELS)

    def scatter(src, dst, peer, pos, rows):
        group = []
        for d in range(1, RING):
            to = lax.rem(pos + d, RING)
            group.append(
                send(src.at[pl.ds(pl.multiple_of(to * rows, rows), rows)], dst.at[d], peer(d))
            )
        return group

    def spread(src, dst, peer):
        return [send(src, dst.at[d], peer(d)) for d in range(1, RING)]

    def own_rows(pos, rows):
        return pl.ds(pl.multiple_of(pos * rows, rows), rows)

    def gather(full, peer, pos, rows, start=0):
        at = pl.ds(pl.multiple_of(start + pos * rows, rows), rows)
        return [send(full.at[at], full.at[at], peer(d)) for d in range(1, RING)]

    chosen_rs = scatter(csp, crz, zpeer, z, CUT)

    def ring_step(buf, peer, s):
        if s < 4:
            right = send(buf.at[OWN + s - 1], buf.at[OWN + s], peer(1))
            left = send(buf.at[OWN - s + 1], buf.at[OWN - s], peer(-1))
        else:
            half_rows = N // 2
            right = send(
                buf.at[OWN + 3, pl.ds(0, half_rows)], buf.at[OWN + 4, pl.ds(0, half_rows)], peer(1)
            )
            left = send(
                buf.at[OWN - 3, pl.ds(half_rows, half_rows)],
                buf.at[OWN + 4, pl.ds(half_rows, half_rows)],
                peer(-1),
            )
        return [right, left]

    flying = ring_step(zbuf, zpeer, 1) + ring_step(ybuf, ypeer, 1)
    psp[...] = pick(hot, samples)
    picked_rs = scatter(psp, prz, zpeer, z, CUT)

    def block(r, c, first):
        weights = gauss(ybuf[r, :, N:], zbuf[c, :, N:]).astype(BF16)
        term = bdot(weights, zbuf[c, :, :N])
        if first:
            tot[r] = term
        else:
            tot[r] += term

    is_upper = [(leaf // 2**level) % 2 for level in range(LEVELS)]
    for level in range(LEVELS):
        index = mskel_ref[pl.ds(level, 1), :]
        index = lax.rem(index + N * is_upper[level], 2 * N)
        wide = (iota((2 * N, N), 0) == index) & (column < ranks_ref[0, level + 1])
        onehots[level] = bdot(eye, wide.astype(F32).astype(BF16), NT).astype(BF16)

    def dead_rows(x, row0, rank):
        rows = x.shape[0]
        gone = iota((rows, AUG), 0) + row0 >= rank
        at = iota((rows, AUG), 1)
        x = jnp.where(gone & (at == 64), DEAD, x)
        return jnp.where(gone & (at == 67), 1.0, x).astype(BF16)

    seen = set()
    known = [OWN]
    for s in range(5):
        if s > 0:
            arrive(flying)
            known = list(range(max(0, OWN - s), OWN + s + 1))
        if s < 4:
            flying = ring_step(zbuf, zpeer, s + 1) + ring_step(ybuf, ypeer, s + 1) if s > 0 else flying
        if s == 1:
            arrive(chosen_rs)
            total = csp[own_rows(z, CUT), :].astype(F32)
            for d in range(1, RING):
                total += crz[d].astype(F32)
            csum[...] = total.astype(BF16)
            chosen_ag = spread(csum, cry, ypeer)
        if s == 2:
            arrive(chosen_ag)
            total = csum[...].astype(F32)
            for d in range(1, RING):
                total += cry[d].astype(F32)
            cz[...] = dead_rows(total, z * CUT, ranks_ref[0, 0])
            och[0, own_rows(z, CUT), :] = cz[...]
            chosen_all = gather(och.at[0], zpeer, z, CUT)
        if s == 4:
            arrive(picked_rs)
            total = psp[own_rows(z, CUT), :]
            for d in range(1, RING):
                total += prz[d]
            for c in range(RING):
                weights = gauss(cz[...], zbuf[c, :, N:]).astype(BF16)
                total -= bdot(weights, zbuf[c, :, :N])
            psum[...] = total
            picked_ag = spread(psum, pry, ypeer)
        for c in known:
            for r in known:
                if (r, c) not in seen:
                    block(r, c, all((r, k) not in seen for k in range(RING)))
                    seen.add((r, c))

    sh, sl = split2(samples)
    mt = bdot(omega_t, sh) + bdot(omega_t, sl)
    for r in range(RING):
        th, tl = split2(tot[r])
        turned = ybuf[r, :, :N]
        mt -= bdot(turned, th) + bdot(turned, tl)
    mtp[...] = mt
    halves = ((0, z, zpeer, ypeer), (N // 2, y, ypeer, zpeer))
    piece = N // 2 // RING
    stage = []
    for i, (start, pos, first, second) in enumerate(halves):
        stage += scatter(mtp.at[pl.ds(start, N // 2)], mr1.at[i], first, pos, piece)

    arrive(picked_ag)
    total = psum[...]
    for d in range(1, RING):
        total += pry[d]
    opk[0, own_rows(z, CUT), :] = total
    picked_all = gather(opk.at[0], zpeer, z, CUT)

    arrive(stage)
    stage = []
    for i, (start, pos, first, second) in enumerate(halves):
        at = pl.ds(pl.multiple_of(start + pos * piece, piece), piece)
        total = mtp[at, :]
        for d in range(1, RING):
            total += mr1[i, d]
        ms1[i] = total
        stage += spread(ms1.at[i], mr2.at[i], second)
    arrive(stage)
    stage = []
    for i, (start, pos, first, second) in enumerate(halves):
        total = ms1[i]
        for d in range(1, RING):
            total += mr2[i, d]
        at = pl.ds(pl.multiple_of(start + pos * piece, piece), piece)
        mfull[at, :] = total
        stage += gather(mfull, first, pos, piece, start)

    arrive(chosen_all)
    arrive(picked_all)

    def swap(level):
        return [
            send(och.at[level], xch.at[level], partners[level]),
            send(opk.at[level], xpk.at[level], partners[level]),
        ]

    early = swap(0)

    hr = N // 2
    flows = []

    def sum_step(s):
        if s > 0:
            arrive(flows[-1])
            if s == 1:
                tot[OWN - 3, :hr] += rsb[0, 0, :hr]
                tot[OWN + 3, hr:] += rsb[1, 0, hr:]
            else:
                tot[OWN - 4 + s] += rsb[0, s - 1]
                tot[OWN + 4 - s] += rsb[1, s - 1]
        if s == 0:
            lower, upper = pl.ds(0, hr), pl.ds(hr, hr)
            flows.append([
                send(tot.at[OWN + 4, lower], rsb.at[0, 0, lower], ypeer(1)),
                send(tot.at[OWN + 4, upper], rsb.at[1, 0, upper], ypeer(-1)),
            ])
        elif s < 4:
            flows.append([
                send(tot.at[OWN - 4 + s], rsb.at[0, s], ypeer(1)),
                send(tot.at[OWN + 4 - s], rsb.at[1, s], ypeer(-1)),
            ])

    sum_step(0)
    picked = opk[0]
    inverse = ridge_inverse(picked)
    turned_leaf = dot3(inverse, picked)
    arrive(stage)
    ocm[0] = dot6(inverse, dot6(picked, mfull[...], NT))
    late = send(ocm.at[0], xcm.at[0], partners[0])

    row = iota((AUG, AUG), 0)
    col = iota((AUG, AUG), 1)
    turn = jnp.where((row >= 64) & (row < 67), row + 3, jnp.where((row >= 67) & (row < 70), row - 3, row))
    turn = (turn == col).astype(F32).astype(BF16)

    for level in range(1, LEVELS + 1):
        last = level - 1
        sum_step(level)
        early[0].wait_recv()
        own_f, other_f = och[last], xch[last]
        own_g = bdot(own_f, turn).astype(BF16)
        other_g = bdot(other_f, turn).astype(BF16)
        coupling = gauss(own_f, other_g)
        coupling_t = gauss(other_f, own_g)
        coup_out[0, last] = coupling
        onehot = onehots[last]
        fresh = bdot(onehot[:, :N], own_f) + bdot(onehot[:, N:], other_f)
        och[level] = dead_rows(fresh, 0, ranks_ref[0, level])
        if level == LEVELS:
            sum_step(4)
            resid = samples_ref[...] - tot[OWN]
            leaf_out[...] = dot3(resid, turned_leaf, NT)
        early[1].wait_recv()
        late.wait_recv()
        co[:N] = ocm[last]
        co[N:] = xcm[last]
        cy[:N] = opk[last] - dot3(coupling, xcm[last])
        cy[N:] = xpk[last] - dot3(coupling_t, ocm[last])
        cand = cy[...]
        picked = pick(onehot, cand)
        opk[level] = picked
        if level < LEVELS:
            early = swap(level)
        inverse = ridge_inverse(picked)
        weight = dot6(dot6(picked, cand, NT), co[...])
        compressed = dot6(inverse, weight)
        if level < LEVELS:
            ocm[level] = compressed
            late = send(ocm.at[level], xcm.at[level], partners[level])
        else:
            top_out[0] = compressed
        interp = dot3(cand, dot3(inverse, picked), NT)
        at = is_upper[last] * N
        node_out[0, last, pl.ds(pl.multiple_of(at, N), N), :] = interp[:N]
        node_out[0, last, pl.ds(pl.multiple_of(N - at, N), N), :] = interp[N:]

    for copy in copies:
        copy.wait_send()


N_COPIES = 16 + 6 * (RING - 1) + 6 * (RING - 1) + 8 + 3 * LEVELS


def shards(points, omega, samples, ranks, leaf_skeleton, merge_skeleton):
    vmem = pl.BlockSpec(memory_space=pltpu.VMEM)
    return pl.pallas_call(
        body,
        out_shape=(
            jax.ShapeDtypeStruct((N, N), F32),
            jax.ShapeDtypeStruct((1, LEVELS, 2 * N, N), F32),
            jax.ShapeDtypeStruct((1, LEVELS, N, N), F32),
            jax.ShapeDtypeStruct((1, N, N), F32),
        ),
        in_specs=[vmem] * 5 + [pl.BlockSpec(memory_space=pltpu.SMEM)],
        out_specs=(vmem,) * 4,
        scratch_shapes=[
            pltpu.VMEM((RING, N, N + AUG), BF16),
            pltpu.VMEM((RING, N, N + AUG), BF16),
            pltpu.VMEM((RING, N, N), F32),
            pltpu.VMEM((2, 4, N, N), F32),
            pltpu.VMEM((N, AUG), F32),
            pltpu.VMEM((N, AUG), BF16),
            pltpu.VMEM((RING, CUT, AUG), BF16),
            pltpu.VMEM((CUT, AUG), BF16),
            pltpu.VMEM((RING, CUT, AUG), BF16),
            pltpu.VMEM((CUT, AUG), BF16),
            pltpu.VMEM((LEVELS + 1, N, AUG), BF16),
            pltpu.VMEM((LEVELS, N, AUG), BF16),
            pltpu.VMEM((N, N), F32),
            pltpu.VMEM((RING, CUT, N), F32),
            pltpu.VMEM((CUT, N), F32),
            pltpu.VMEM((RING, CUT, N), F32),
            pltpu.VMEM((LEVELS + 1, N, N), F32),
            pltpu.VMEM((LEVELS, N, N), F32),
            pltpu.VMEM((N, N), F32),
            pltpu.VMEM((2, RING, CUT // 2, N), F32),
            pltpu.VMEM((2, CUT // 2, N), F32),
            pltpu.VMEM((2, RING, CUT // 2, N), F32),
            pltpu.VMEM((N, N), F32),
            pltpu.VMEM((LEVELS, N, N), F32),
            pltpu.VMEM((LEVELS, N, N), F32),
            pltpu.VMEM((LEVELS, N, 2 * N), BF16),
            pltpu.VMEM((2 * N, N), F32),
            pltpu.VMEM((2 * N, N), F32),
            pltpu.SemaphoreType.DMA((N_COPIES,)),
            pltpu.SemaphoreType.DMA((N_COPIES,)),
        ],
        compiler_params=pltpu.CompilerParams(
            collective_id=0, has_side_effects=True, vmem_limit_bytes=56 * 2**20
        ),
    )(omega, points, samples, leaf_skeleton, merge_skeleton[0], ranks)


def solution(mesh):
    in_specs = (
        P(("leaf", "sub"), None),
        P(("leaf", "sub"), None),
        P(("leaf", "sub"), None),
        P("leaf", None),
        P("leaf", None),
        P("leaf", None, None),
    )
    out_specs = (
        P(("leaf", "sub"), None),
        P("leaf", None, None, None),
        P("leaf", None, None, None),
        P("leaf", None, None),
    )
    return jax.shard_map(shards, mesh=mesh, in_specs=in_specs, out_specs=out_specs, check_vma=False)
```

```python
import jax
import jax.numpy as jnp
from jax import lax
from jax.experimental import pallas as pl
from jax.experimental.pallas import tpu as pltpu
from jax.sharding import PartitionSpec as P

F32 = jnp.float32
BF16 = jnp.bfloat16
RING = 8
N = 256
AUG = 128
CUT = N // RING
LEVELS = 3
OWN = RING // 2 - 1
NN = ((1,), (0,))
NT = ((1,), (1,))
TN = ((0,), (0,))
DEAD = -1e30
MESH = pl.DeviceIdType.MESH

SPAN = N + 1.0
SIGMA = (SPAN + 1.0) / (SPAN - 1.0)
CHEB = 2.0 * SIGMA * SIGMA - 1.0
ALPHA = 8.0 * (SPAN + 1.0) / ((SPAN - 1.0) ** 2 * CHEB)
BETA = 8.0 / ((SPAN - 1.0) ** 2 * CHEB)
RATES = []
RHO = 1.0 / CHEB
for _ in range(6):
    RATES.append(2.0 / (2.0 - RHO * RHO))
    RHO = RHO * RHO / (2.0 - RHO * RHO)


def bdot(a, b, dims=NN):
    return lax.dot_general(a, b, (dims, ((), ())), preferred_element_type=F32)


def split2(x):
    hi = x.astype(BF16)
    return hi, (x - hi.astype(F32)).astype(BF16)


def split3(x):
    hi = x.astype(BF16)
    rest = x - hi.astype(F32)
    mid = rest.astype(BF16)
    return hi, mid, (rest - mid.astype(F32)).astype(BF16)


def dot3(a, b, dims=NN):
    ah, al = split2(a)
    bh, bl = split2(b)
    return bdot(ah, bh, dims) + (bdot(ah, bl, dims) + bdot(al, bh, dims))


def pick(onehot, x, dims=NN):
    hi, mid, lo = split3(x)
    return bdot(onehot, hi, dims) + bdot(onehot, mid, dims) + bdot(onehot, lo, dims)


def dot6(a, b, dims=NN):
    return lax.dot_general(
        a, b, (dims, ((), ())), precision=lax.Precision.HIGHEST, preferred_element_type=F32
    )


def iota(shape, dim):
    return lax.broadcasted_iota(jnp.int32, shape, dim)


def ridge_inverse(p):
    gram = dot6(p, p, NT)
    inv_shift = 1.0 / (jnp.sum(p * p) / N + 1e-06)
    eye = (iota((N, N), 0) == iota((N, N), 1)).astype(F32)
    b = gram * inv_shift + eye
    x = ALPHA * eye - BETA * b
    e = eye - dot3(b, x)
    for w in RATES:
        eh, el = split2(e)
        xh, xl = split2(x)
        e2 = bdot(eh, eh) + (bdot(eh, el) + bdot(el, eh))
        x = w * (x + (bdot(xh, eh) + (bdot(xh, el) + bdot(xl, eh))))
        e = (1.0 - w) * eye + w * e2
    x = x + dot6(x, eye - dot6(b, x))
    return x * inv_shift


def gauss(left_f, right_g):
    return jnp.exp(bdot(left_f, right_g, NT) * 0.0625)


def body(
    omega_ref, points_ref, samples_ref, skel_ref, mskel_ref, ranks_ref,
    diag_out, turn_out, node_out, coup_out, top_out,
    zbuf, ybuf, tot, rsb,
    csp, crz, cry, cz, och, xch,
    psp, prz, pry, opk, xpk,
    mtp, mr1, mr2, mfull, ocm, xcm, onehots, cy, co,
    send_sem, recv_sem,
):
    sub = lax.axis_index("sub")
    leaf = lax.axis_index("leaf")
    z = sub // RING
    y = sub % RING

    def zpeer(d):
        return {"sub": lax.rem(z + d + RING, RING) * RING + y}

    def ypeer(d):
        return {"sub": z * RING + lax.rem(y + d + RING, RING)}

    barrier = pltpu.get_barrier_semaphore()
    for d in range(1, RING):
        pl.semaphore_signal(barrier, inc=1, device_id=zpeer(d), device_id_type=MESH)
        pl.semaphore_signal(barrier, inc=1, device_id=ypeer(d), device_id_type=MESH)
    partners = []
    for level in range(LEVELS):
        bit = (leaf // 2**level) % 2
        partners.append({"leaf": leaf + (1 - 2 * bit) * 2**level})
        pl.semaphore_signal(barrier, inc=1, device_id=partners[-1], device_id_type=MESH)

    copies = []

    def send(src, dst, device):
        at = len(copies)
        copy = pltpu.make_async_remote_copy(
            src_ref=src, dst_ref=dst, send_sem=send_sem.at[at], recv_sem=recv_sem.at[at],
            device_id=device, device_id_type=MESH,
        )
        copy.start()
        copies.append(copy)
        return copy

    def arrive(group):
        for copy in group:
            copy.wait_recv()

    eye = (iota((N, N), 0) == iota((N, N), 1)).astype(BF16)
    padded = jnp.concatenate([points_ref[...], jnp.zeros((AUG - 64, N), BF16)], axis=0)
    plain = bdot(eye, padded, NT)
    half = -0.5 * jnp.sum(plain * plain, axis=1, keepdims=True)
    h1, h2, h3 = (piece.astype(F32) for piece in split3(half))
    lane = iota((N, AUG), 1)

    def place(at, other):
        out = jnp.where((lane >= other) & (lane < other + 3), 1.0, plain)
        for i, piece in enumerate((h1, h2, h3)):
            out = jnp.where(lane == at + i, piece, out)
        return out.astype(BF16)

    feat = place(64, 67)
    omega = omega_ref[...]
    samples = samples_ref[...]
    omega_t = bdot(eye, omega, NT).astype(BF16)
    zbuf[OWN, :, :N] = omega
    zbuf[OWN, :, N:] = place(67, 64)
    ybuf[OWN, :, :N] = omega_t
    ybuf[OWN, :, N:] = feat
    column = iota((1, N), 1)
    offset = skel_ref[...] - sub * N
    hits = (iota((N, N), 0) == offset) & (column < ranks_ref[0, 0])
    hits = hits.astype(F32).astype(BF16)
    hot = bdot(eye, hits, NT).astype(BF16)
    csp[...] = bdot(hot, feat).astype(BF16)

    pl.semaphore_wait(barrier, 2 * (RING - 1) + LEVELS)

    def scatter(src, dst, peer, pos, rows):
        group = []
        for d in range(1, RING):
            to = lax.rem(pos + d, RING)
            group.append(
                send(src.at[pl.ds(pl.multiple_of(to * rows, rows), rows)], dst.at[d], peer(d))
            )
        return group

    def spread(dst, peer, pos):
        return [send(dst.at[pos], dst.at[pos], peer(d)) for d in range(1, RING)]

    def own_rows(pos, rows):
        return pl.ds(pl.multiple_of(pos * rows, rows), rows)

    def gather(full, peer, pos, rows, start=0):
        at = pl.ds(pl.multiple_of(start + pos * rows, rows), rows)
        return [send(full.at[at], full.at[at], peer(d)) for d in range(1, RING)]

    chosen_rs = scatter(csp, crz, zpeer, z, CUT)

    hr = N // 2
    top, bottom = pl.ds(0, hr), pl.ds(hr, hr)

    def right(axis, s, part):
        buf, peer = axis
        at = top if part == 0 else bottom
        return send(buf.at[OWN + s - 1, at], buf.at[OWN + s, at], peer(1))

    def left(axis, s, part):
        buf, peer = axis
        at = top if part == 0 else bottom
        to = OWN - s if s < 4 else OWN + 4
        return send(buf.at[OWN - s + 1, at], buf.at[to, at], peer(-1))

    axes = ((zbuf, zpeer), (ybuf, ypeer))
    flying = {}

    def launch(axis, s, part):
        if s < 4 or part == 0:
            flying[axis, 0, s, part] = right(axes[axis], s, part)
        if s < 4 or part == 1:
            flying[axis, 1, s, part] = left(axes[axis], s, part)

    for part in range(2):
        for axis in range(2):
            launch(axis, 1, part)

    def block(r, c, first):
        weights = gauss(ybuf[r, :, N:], zbuf[c, :, N:]).astype(BF16)
        term = bdot(weights, zbuf[c, :, :N])
        if first:
            tot[r] = term
        else:
            tot[r] += term

    is_upper = [(leaf // 2**level) % 2 for level in range(LEVELS)]
    for level in range(LEVELS):
        index = mskel_ref[level]
        index = lax.rem(index + N * is_upper[level], 2 * N)
        wide = (iota((2 * N, N), 0) == index) & (column < ranks_ref[0, level + 1])
        onehots[level] = bdot(eye, wide.astype(F32).astype(BF16), NT).astype(BF16)

    def dead_rows(x, row0, rank):
        rows = x.shape[0]
        gone = iota((rows, AUG), 0) + row0 >= rank
        at = iota((rows, AUG), 1)
        x = jnp.where(gone & (at == 64), DEAD, x)
        return jnp.where(gone & (at == 67), 1.0, x).astype(BF16)

    def total_of(dst):
        total = dst[0].astype(F32)
        for d in range(1, RING):
            total += dst[d].astype(F32)
        return total

    seen = set()
    todo = [(OWN, OWN)]

    def work(pairs):
        for r, c in pairs:
            block(r, c, all((r, k) not in seen for k in range(RING)))
            seen.add((r, c))

    for s in range(1, 5):
        for part in range(2):
            for axis in range(2):
                for way in range(2):
                    copy = flying.pop((axis, way, s, part), None)
                    if copy is not None:
                        copy.wait_recv()
                        if s < 3 or (s == 3 and part == way):
                            if way == 0:
                                flying[axis, 0, s + 1, part] = right(axes[axis], s + 1, part)
                            else:
                                flying[axis, 1, s + 1, part] = left(axes[axis], s + 1, part)
            if s == 1 and part == 1:
                psp[...] = pick(hot, samples)
                picked_rs = scatter(psp, prz, zpeer, z, CUT)
            if s == 2 and part == 0:
                arrive(chosen_rs)
                total = csp[own_rows(z, CUT), :].astype(F32)
                for d in range(1, RING):
                    total += crz[d].astype(F32)
                cry[y] = total.astype(BF16)
                chosen_ag = spread(cry, ypeer, y)
            if s == 3 and part == 1:
                arrive(chosen_ag)
                cz[...] = dead_rows(total_of(cry), z * CUT, ranks_ref[0, 0])
                och[0, own_rows(z, CUT), :] = cz[...]
                chosen_all = gather(och.at[0], zpeer, z, CUT)
            cut = len(todo) // 2
            work(todo[:cut] if part == 0 else todo)
            todo = todo[cut:] if part == 0 else []
        known = range(max(0, OWN - s), OWN + s + 1)
        todo = [(r, c) for c in known for r in known if (r, c) not in seen]

    arrive(picked_rs)
    total = psp[own_rows(z, CUT), :]
    for d in range(1, RING):
        total += prz[d]
    for c in range(RING):
        weights = gauss(cz[...], zbuf[c, :, N:]).astype(BF16)
        total -= bdot(weights, zbuf[c, :, :N])
    pry[y] = total
    picked_ag = spread(pry, ypeer, y)
    work(todo)

    flows = []

    def sum_step(s):
        if s > 0:
            arrive(flows[-1])
            if s == 1:
                tot[OWN - 3, :hr] += rsb[0, 0, :hr]
                tot[OWN + 3, hr:] += rsb[1, 0, hr:]
            else:
                tot[OWN - 4 + s] += rsb[0, s - 1]
                tot[OWN + 4 - s] += rsb[1, s - 1]
        if s == 0:
            flows.append([
                send(tot.at[OWN + 4, top], rsb.at[0, 0, top], ypeer(1)),
                send(tot.at[OWN + 4, bottom], rsb.at[1, 0, bottom], ypeer(-1)),
            ])
        elif s < 4:
            flows.append([
                send(tot.at[OWN - 4 + s], rsb.at[0, s], ypeer(1)),
                send(tot.at[OWN + 4 - s], rsb.at[1, s], ypeer(-1)),
            ])

    sum_step(0)
    sh, sl = split2(samples)
    mt = bdot(omega_t, sh) + bdot(omega_t, sl)
    for r in range(RING):
        th, tl = split2(tot[r])
        turned = ybuf[r, :, :N]
        mt -= bdot(turned, th) + bdot(turned, tl)
    mtp[...] = mt
    halves = ((0, z, y, zpeer, ypeer), (hr, y, z, ypeer, zpeer))
    piece = hr // RING
    stage = []
    for i, (start, pos, other, first, second) in enumerate(halves):
        stage += scatter(mtp.at[pl.ds(start, hr)], mr1.at[i], first, pos, piece)

    arrive(picked_ag)
    opk[0, own_rows(z, CUT), :] = total_of(pry)
    picked_all = gather(opk.at[0], zpeer, z, CUT)

    arrive(stage)
    stage = []
    for i, (start, pos, other, first, second) in enumerate(halves):
        at = pl.ds(pl.multiple_of(start + pos * piece, piece), piece)
        total = mtp[at, :]
        for d in range(1, RING):
            total += mr1[i, d]
        mr2[i, other] = total
        stage += spread(mr2.at[i], second, other)
    arrive(stage)
    stage = []
    for i, (start, pos, other, first, second) in enumerate(halves):
        at = pl.ds(pl.multiple_of(start + pos * piece, piece), piece)
        mfull[at, :] = total_of(mr2.at[i])
        stage += gather(mfull, first, pos, piece, start)

    arrive(chosen_all)
    arrive(picked_all)

    core = leaf % 2
    mate = partners[0]
    mine = pl.ds(pl.multiple_of(core * hr, hr), hr)

    def offer(src, dst, level):
        if level == 0:
            return [send(src.at[0], dst.at[0], mate)]
        return [send(src.at[level, mine], dst.at[level, mine], partners[level])]

    def accept(group, dst, level):
        arrive(group)
        if level > 0:
            return [send(dst.at[level, mine], dst.at[level, mine], mate)]
        return []

    def swap(level):
        return [offer(och, xch, level), offer(opk, xpk, level)]

    early = swap(0)
    picked = opk[0]
    inverse = ridge_inverse(picked)
    turn_out[...] = dot3(inverse, picked)
    arrive(stage)
    ocm[0] = dot6(inverse, dot6(picked, mfull[...], NT))
    late = offer(ocm, xcm, 0)

    row = iota((AUG, AUG), 0)
    col = iota((AUG, AUG), 1)
    turn = jnp.where((row >= 64) & (row < 67), row + 3, jnp.where((row >= 67) & (row < 70), row - 3, row))
    turn = (turn == col).astype(F32).astype(BF16)

    for level in range(1, LEVELS + 1):
        last = level - 1
        handed = accept(early[0], xch, last) + accept(early[1], xpk, last)
        arrive(handed[:1])
        own_f, other_f = och[last], xch[last]
        own_g = bdot(own_f, turn).astype(BF16)
        other_g = bdot(other_f, turn).astype(BF16)
        coupling = gauss(own_f, other_g)
        coupling_t = gauss(other_f, own_g)
        coup_out[0, last] = coupling
        onehot = onehots[last]
        fresh = bdot(onehot[:, :N], own_f) + bdot(onehot[:, N:], other_f)
        och[level] = dead_rows(fresh, 0, ranks_ref[0, level])
        arrive(handed[1:])
        arrive(accept(late, xcm, last))
        co[:N] = ocm[last]
        co[N:] = xcm[last]
        cy[:N] = opk[last] - dot3(coupling, xcm[last])
        cy[N:] = xpk[last] - dot3(coupling_t, ocm[last])
        cand = cy[...]
        picked = pick(onehot, cand)
        opk[level] = picked
        if level < LEVELS:
            early = swap(level)
        sum_step(level)
        inverse = ridge_inverse(picked)
        weight = dot6(dot6(picked, cand, NT), co[...])
        compressed = dot6(inverse, weight)
        if level < LEVELS:
            ocm[level] = compressed
            late = offer(ocm, xcm, level)
        else:
            top_out[0] = compressed
        interp = dot3(cand, dot3(inverse, picked), NT)
        at = is_upper[last] * N
        node_out[0, last, pl.ds(pl.multiple_of(at, N), N), :] = interp[:N]
        node_out[0, last, pl.ds(pl.multiple_of(N - at, N), N), :] = interp[N:]

    sum_step(4)
    diag_out[...] = tot[OWN]
    for copy in copies:
        copy.wait_send()


def finish(samples_ref, diag_ref, turn_ref, node_ref, coup_ref, top_ref, leaf_out, node_out, coup_out, top_out, sems):
    moves = [
        pltpu.make_async_copy(src, dst, sems.at[i])
        for i, (src, dst) in enumerate(((node_ref, node_out), (coup_ref, coup_out), (top_ref, top_out)))
    ]
    for move in moves:
        move.start()
    leaf_out[...] = dot3(samples_ref[...] - diag_ref[...], turn_ref[...], NT)
    for move in moves:
        move.wait()


N_COPIES = 28 + 6 * (RING - 1) + 6 * (RING - 1) + 8 + 3 + 6 * (LEVELS - 1)


def shards(points, omega, samples, ranks, leaf_skeleton, merge_skeleton):
    vmem = pl.BlockSpec(memory_space=pltpu.VMEM)
    parts = pl.pallas_call(
        body,
        out_shape=(
            jax.ShapeDtypeStruct((N, N), F32),
            jax.ShapeDtypeStruct((N, N), F32),
            jax.ShapeDtypeStruct((1, LEVELS, 2 * N, N), F32),
            jax.ShapeDtypeStruct((1, LEVELS, N, N), F32),
            jax.ShapeDtypeStruct((1, N, N), F32),
        ),
        in_specs=[vmem] * 5 + [pl.BlockSpec(memory_space=pltpu.SMEM)],
        out_specs=(vmem,) * 5,
        scratch_shapes=[
            pltpu.VMEM((RING, N, N + AUG), BF16),
            pltpu.VMEM((RING, N, N + AUG), BF16),
            pltpu.VMEM((RING, N, N), F32),
            pltpu.VMEM((2, 4, N, N), F32),
            pltpu.VMEM((N, AUG), BF16),
            pltpu.VMEM((RING, CUT, AUG), BF16),
            pltpu.VMEM((RING, CUT, AUG), BF16),
            pltpu.VMEM((CUT, AUG), BF16),
            pltpu.VMEM((LEVELS + 1, N, AUG), BF16),
            pltpu.VMEM((LEVELS, N, AUG), BF16),
            pltpu.VMEM((N, N), F32),
            pltpu.VMEM((RING, CUT, N), F32),
            pltpu.VMEM((RING, CUT, N), F32),
            pltpu.VMEM((LEVELS + 1, N, N), F32),
            pltpu.VMEM((LEVELS, N, N), F32),
            pltpu.VMEM((N, N), F32),
            pltpu.VMEM((2, RING, CUT // 2, N), F32),
            pltpu.VMEM((2, RING, CUT // 2, N), F32),
            pltpu.VMEM((N, N), F32),
            pltpu.VMEM((LEVELS, N, N), F32),
            pltpu.VMEM((LEVELS, N, N), F32),
            pltpu.VMEM((LEVELS, N, 2 * N), BF16),
            pltpu.VMEM((2 * N, N), F32),
            pltpu.VMEM((2 * N, N), F32),
            pltpu.SemaphoreType.DMA((N_COPIES,)),
            pltpu.SemaphoreType.DMA((N_COPIES,)),
        ],
        compiler_params=pltpu.CompilerParams(
            collective_id=0, has_side_effects=True, vmem_limit_bytes=40 * 2**20
        ),
    )(omega, points.T, samples, leaf_skeleton, merge_skeleton.transpose(1, 0, 2), ranks)
    hold = pl.BlockSpec(memory_space=pl.ANY)
    return pl.pallas_call(
        finish,
        out_shape=(jax.ShapeDtypeStruct((N, N), F32),)
        + tuple(jax.ShapeDtypeStruct(part.shape, F32) for part in parts[2:]),
        in_specs=[vmem] * 3 + [hold] * 3,
        out_specs=(vmem,) + (hold,) * 3,
        scratch_shapes=[pltpu.SemaphoreType.DMA((3,))],
        compiler_params=pltpu.CompilerParams(vmem_limit_bytes=16 * 2**20),
    )(samples, *parts)


def solution(mesh):
    in_specs = (
        P(("leaf", "sub"), None),
        P(("leaf", "sub"), None),
        P(("leaf", "sub"), None),
        P("leaf", None),
        P("leaf", None),
        P("leaf", None, None),
    )
    out_specs = (
        P(("leaf", "sub"), None),
        P("leaf", None, None, None),
        P("leaf", None, None, None),
        P("leaf", None, None),
    )
    return jax.shard_map(shards, mesh=mesh, in_specs=in_specs, out_specs=out_specs, check_vma=False)
```

```python
import jax
import jax.numpy as jnp
from jax import lax
from jax.experimental import pallas as pl
from jax.experimental.pallas import tpu as pltpu
from jax.sharding import PartitionSpec as P

F32 = jnp.float32
BF16 = jnp.bfloat16
RING = 8
N = 256
AUG = 128
CUT = N // RING
PIECES = 4
LEVELS = 3
OWN = RING // 2 - 1
NN = ((1,), (0,))
NT = ((1,), (1,))
TN = ((0,), (0,))
DEAD = -1e30
MESH = pl.DeviceIdType.MESH

SPAN = N + 1.0
SIGMA = (SPAN + 1.0) / (SPAN - 1.0)
CHEB = 2.0 * SIGMA * SIGMA - 1.0
ALPHA = 8.0 * (SPAN + 1.0) / ((SPAN - 1.0) ** 2 * CHEB)
BETA = 8.0 / ((SPAN - 1.0) ** 2 * CHEB)
RATES = []
RHO = 1.0 / CHEB
for _ in range(6):
    RATES.append(2.0 / (2.0 - RHO * RHO))
    RHO = RHO * RHO / (2.0 - RHO * RHO)


def bdot(a, b, dims=NN):
    return lax.dot_general(a, b, (dims, ((), ())), preferred_element_type=F32)


def split2(x):
    hi = x.astype(BF16)
    return hi, (x - hi.astype(F32)).astype(BF16)


def split3(x):
    hi = x.astype(BF16)
    rest = x - hi.astype(F32)
    mid = rest.astype(BF16)
    return hi, mid, (rest - mid.astype(F32)).astype(BF16)


def dot3(a, b, dims=NN):
    ah, al = split2(a)
    bh, bl = split2(b)
    return bdot(ah, bh, dims) + (bdot(ah, bl, dims) + bdot(al, bh, dims))


def pick(onehot, x, dims=NN):
    hi, mid, lo = split3(x)
    return bdot(onehot, hi, dims) + bdot(onehot, mid, dims) + bdot(onehot, lo, dims)


def dot6(a, b, dims=NN):
    return lax.dot_general(
        a, b, (dims, ((), ())), precision=lax.Precision.HIGHEST, preferred_element_type=F32
    )


def iota(shape, dim):
    return lax.broadcasted_iota(jnp.int32, shape, dim)


def ridge_factor(p):
    gram = dot6(p, p, NT)
    inv_shift = 1.0 / (jnp.sum(p * p) / N + 1e-06)
    eye = (iota((N, N), 0) == iota((N, N), 1)).astype(F32)
    b = gram * inv_shift + eye
    x = ALPHA * eye - BETA * b
    e = eye - dot3(b, x)
    for step, w in enumerate(RATES):
        if step < 4:
            eh, el = split2(e)
            xh, xl = split2(x)
            e2 = bdot(eh, eh) + (bdot(eh, el) + bdot(el, eh))
            x = w * (x + (bdot(xh, eh) + (bdot(xh, el) + bdot(xl, eh))))
        else:
            eh = e.astype(BF16)
            e2 = bdot(eh, eh)
            x = w * (x + bdot(x.astype(BF16), eh))
        e = (1.0 - w) * eye + w * e2
    return b, x, inv_shift


def ridge_solve(factor, right):
    b, x, inv_shift = factor
    first = dot3(x, right)
    return (first + dot3(x, right - dot6(b, first))) * inv_shift


def gauss(left_f, right_g):
    return jnp.exp(bdot(left_f, right_g, NT) * 0.0625)


def body(
    omega_hbm, points_hbm, samples_hbm, skel_hbm, mskel_hbm, ranks_hbm,
    diag_hbm, turn_hbm, node_hbm, coup_hbm, top_hbm,
    zbuf, ybuf, tot, rsb,
    csp, crz, cry, cz, och, xch,
    psp, prz, pry, opk, xpk,
    mtp, mr1, mr2, mfull, ocm, xcm, onehots, cy, co,
    points_ref, omega_ref, skel_ref, ranks_ref, samples_ref, mskel_ref, load_sem,
    turn_out, node_out, coup_out, top_out, store_sem, send_sem, recv_sem,
):
    loads = [
        pltpu.make_async_copy(src, dst, load_sem.at[i])
        for i, (src, dst) in enumerate((
            (points_hbm, points_ref), (omega_hbm, omega_ref), (skel_hbm, skel_ref),
            (ranks_hbm, ranks_ref), (samples_hbm, samples_ref), (mskel_hbm, mskel_ref),
        ))
    ]
    for load in loads:
        load.start()
    stores = []

    def store(src, dst):
        stores.append(pltpu.make_async_copy(src, dst, store_sem.at[len(stores)]))
        stores[-1].start()

    sub = lax.axis_index("sub")
    leaf = lax.axis_index("leaf")
    z = sub // RING
    y = sub % RING

    def zpeer(d):
        return {"sub": lax.rem(z + d + RING, RING) * RING + y}

    def ypeer(d):
        return {"sub": z * RING + lax.rem(y + d + RING, RING)}

    barrier = pltpu.get_barrier_semaphore()
    for d in range(1, RING):
        pl.semaphore_signal(barrier, inc=1, device_id=zpeer(d), device_id_type=MESH)
        pl.semaphore_signal(barrier, inc=1, device_id=ypeer(d), device_id_type=MESH)
    partners = []
    for level in range(LEVELS):
        bit = (leaf // 2**level) % 2
        partners.append({"leaf": leaf + (1 - 2 * bit) * 2**level})
        pl.semaphore_signal(barrier, inc=1, device_id=partners[-1], device_id_type=MESH)

    copies = []

    def send(src, dst, device):
        at = len(copies)
        copy = pltpu.make_async_remote_copy(
            src_ref=src, dst_ref=dst, send_sem=send_sem.at[at], recv_sem=recv_sem.at[at],
            device_id=device, device_id_type=MESH,
        )
        copy.start()
        copies.append(copy)
        return copy

    def arrive(group):
        for copy in group:
            copy.wait_recv()

    for load in loads[:4]:
        load.wait()

    eye = (iota((N, N), 0) == iota((N, N), 1)).astype(BF16)
    padded = jnp.concatenate([points_ref[...], jnp.zeros((AUG - 64, N), BF16)], axis=0)
    plain = bdot(eye, padded, NT)
    half = -0.5 * jnp.sum(plain * plain, axis=1, keepdims=True)
    h1, h2, h3 = (piece.astype(F32) for piece in split3(half))
    lane = iota((N, AUG), 1)

    def place(at, other):
        out = jnp.where((lane >= other) & (lane < other + 3), 1.0, plain)
        for i, piece in enumerate((h1, h2, h3)):
            out = jnp.where(lane == at + i, piece, out)
        return out.astype(BF16)

    feat = place(64, 67)
    omega = omega_ref[...]
    omega_t = bdot(eye, omega, NT).astype(BF16)
    zbuf[OWN, :, :N] = omega
    zbuf[OWN, :, N:] = place(67, 64)
    ybuf[OWN, :, :N] = omega_t
    ybuf[OWN, :, N:] = feat
    pl.semaphore_wait(barrier, 2 * (RING - 1) + LEVELS)

    def scatter(src, dst, peer, pos, rows):
        group = []
        for d in range(1, RING):
            to = lax.rem(pos + d, RING)
            group.append(
                send(src.at[pl.ds(pl.multiple_of(to * rows, rows), rows)], dst.at[d], peer(d))
            )
        return group

    def spread(dst, peer, pos):
        return [send(dst.at[pos], dst.at[pos], peer(d)) for d in range(1, RING)]

    def own_rows(pos, rows):
        return pl.ds(pl.multiple_of(pos * rows, rows), rows)

    def gather(full, peer, pos, rows, start=0):
        at = pl.ds(pl.multiple_of(start + pos * rows, rows), rows)
        return [send(full.at[at], full.at[at], peer(d)) for d in range(1, RING)]

    hr = N // 2
    top, bottom = pl.ds(0, hr), pl.ds(hr, hr)

    def right(axis, s, part):
        buf, peer = axis
        at = pl.ds(part * (N // PIECES), N // PIECES)
        return send(buf.at[OWN + s - 1, at], buf.at[OWN + s, at], peer(1))

    def left(axis, s, part):
        buf, peer = axis
        at = pl.ds(part * (N // PIECES), N // PIECES)
        to = OWN - s if s < 4 else OWN + 4
        return send(buf.at[OWN - s + 1, at], buf.at[to, at], peer(-1))

    axes = ((zbuf, zpeer), (ybuf, ypeer))
    ways = (right, left)
    flying = {}

    def launch(axis, way, s, part):
        if s < 4 or part * 2 // PIECES == way:
            flying[axis, way, s, part] = ways[way](axes[axis], s, part)

    for part in range(PIECES):
        for axis in range(2):
            for way in range(2):
                launch(axis, way, 1, part)

    column = iota((1, N), 1)
    offset = skel_ref[...] - sub * N
    hits = (iota((N, N), 0) == offset) & (column < ranks_ref[0, 0])
    hot = bdot(eye, hits.astype(F32).astype(BF16), NT).astype(BF16)
    csp[...] = bdot(hot, feat).astype(BF16)
    chosen_rs = scatter(csp, crz, zpeer, z, CUT)

    def block(r, c, first):
        weights = gauss(ybuf[r, :, N:], zbuf[c, :, N:]).astype(BF16)
        term = bdot(weights, zbuf[c, :, :N])
        if first:
            tot[r] = term
        else:
            tot[r] += term

    loads[5].wait()
    is_upper = [(leaf // 2**level) % 2 for level in range(LEVELS)]
    for level in range(LEVELS):
        index = mskel_ref[level]
        index = lax.rem(index + N * is_upper[level], 2 * N)
        wide = (iota((2 * N, N), 0) == index) & (column < ranks_ref[0, level + 1])
        onehots[level] = bdot(eye, wide.astype(F32).astype(BF16), NT).astype(BF16)

    def dead_rows(x, row0, rank):
        rows = x.shape[0]
        gone = iota((rows, AUG), 0) + row0 >= rank
        at = iota((rows, AUG), 1)
        x = jnp.where(gone & (at == 64), DEAD, x)
        return jnp.where(gone & (at == 67), 1.0, x).astype(BF16)

    def total_of(dst):
        total = dst[0].astype(F32)
        for d in range(1, RING):
            total += dst[d].astype(F32)
        return total

    seen = set()
    todo = [(OWN, OWN)]

    def work(pairs):
        for r, c in pairs:
            block(r, c, all((r, k) not in seen for k in range(RING)))
            seen.add((r, c))

    for s in range(1, 5):
        for part in range(PIECES):
            for axis in range(2):
                for way in range(2):
                    copy = flying.pop((axis, way, s, part), None)
                    if copy is not None:
                        copy.wait_recv()
                        if s < 4:
                            launch(axis, way, s + 1, part)
            if s == 1 and part == PIECES - 1:
                loads[4].wait()
                psp[...] = pick(hot, samples_ref[...])
                picked_rs = scatter(psp, prz, zpeer, z, CUT)
            if s == 2 and part == 0:
                arrive(chosen_rs)
                total = csp[own_rows(z, CUT), :].astype(F32)
                for d in range(1, RING):
                    total += crz[d].astype(F32)
                cry[y] = total.astype(BF16)
                chosen_ag = spread(cry, ypeer, y)
            if s == 3 and part == PIECES - 1:
                arrive(chosen_ag)
                cz[...] = dead_rows(total_of(cry), z * CUT, ranks_ref[0, 0])
                och[0, own_rows(z, CUT), :] = cz[...]
                chosen_all = gather(och.at[0], zpeer, z, CUT)
            cut = len(todo) // (PIECES - part)
            work(todo[:cut])
            todo = todo[cut:]
        known = range(max(0, OWN - s), OWN + s + 1)
        todo = [(r, c) for c in known for r in known if (r, c) not in seen]

    arrive(picked_rs)
    total = psp[own_rows(z, CUT), :]
    for d in range(1, RING):
        total += prz[d]
    for c in range(RING):
        weights = gauss(cz[...], zbuf[c, :, N:]).astype(BF16)
        total -= bdot(weights, zbuf[c, :, :N])
    pry[y] = total
    picked_ag = spread(pry, ypeer, y)
    work(todo)

    flows = []

    def sum_step(s):
        if s > 0:
            arrive(flows[-1])
            if s == 1:
                tot[OWN - 3, :hr] += rsb[0, 0, :hr]
                tot[OWN + 3, hr:] += rsb[1, 0, hr:]
            else:
                tot[OWN - 4 + s] += rsb[0, s - 1]
                tot[OWN + 4 - s] += rsb[1, s - 1]
        if s == 0:
            flows.append([
                send(tot.at[OWN + 4, top], rsb.at[0, 0, top], ypeer(1)),
                send(tot.at[OWN + 4, bottom], rsb.at[1, 0, bottom], ypeer(-1)),
            ])
        elif s < 4:
            flows.append([
                send(tot.at[OWN - 4 + s], rsb.at[0, s], ypeer(1)),
                send(tot.at[OWN + 4 - s], rsb.at[1, s], ypeer(-1)),
            ])

    sum_step(0)
    sh, sl = split2(samples_ref[...])
    mt = bdot(omega_t, sh) + bdot(omega_t, sl)
    for r in range(RING):
        th, tl = split2(tot[r])
        turned = ybuf[r, :, :N]
        mt -= bdot(turned, th) + bdot(turned, tl)
    mtp[...] = mt
    halves = ((0, z, y, zpeer, ypeer), (hr, y, z, ypeer, zpeer))
    piece = hr // RING
    stage = []
    for i, (start, pos, other, first, second) in enumerate(halves):
        stage += scatter(mtp.at[pl.ds(start, hr)], mr1.at[i], first, pos, piece)

    arrive(picked_ag)
    opk[0, own_rows(z, CUT), :] = total_of(pry)
    picked_all = gather(opk.at[0], zpeer, z, CUT)

    arrive(stage)
    stage = []
    for i, (start, pos, other, first, second) in enumerate(halves):
        at = pl.ds(pl.multiple_of(start + pos * piece, piece), piece)
        total = mtp[at, :]
        for d in range(1, RING):
            total += mr1[i, d]
        mr2[i, other] = total
        stage += spread(mr2.at[i], second, other)
    arrive(stage)
    stage = []
    for i, (start, pos, other, first, second) in enumerate(halves):
        at = pl.ds(pl.multiple_of(start + pos * piece, piece), piece)
        mfull[at, :] = total_of(mr2.at[i])
        stage += gather(mfull, first, pos, piece, start)

    arrive(chosen_all)
    arrive(picked_all)

    core = leaf % 2
    mate = partners[0]
    mine = pl.ds(pl.multiple_of(core * hr, hr), hr)

    def offer(src, dst, level):
        if level == 0:
            return [send(src.at[0], dst.at[0], mate)]
        return [send(src.at[level, mine], dst.at[level, mine], partners[level])]

    def accept(group, dst, level):
        arrive(group)
        if level > 0:
            return [send(dst.at[level, mine], dst.at[level, mine], mate)]
        return []

    def swap(level):
        return [offer(och, xch, level), offer(opk, xpk, level)]

    early = swap(0)
    picked = opk[0]
    factor = ridge_factor(picked)
    arrive(stage)
    ocm[0] = ridge_solve(factor, dot6(picked, mfull[...], NT))
    late = offer(ocm, xcm, 0)
    turn_out[...] = ridge_solve(factor, picked)
    store(turn_out, turn_hbm)

    row = iota((AUG, AUG), 0)
    col = iota((AUG, AUG), 1)
    turn = jnp.where((row >= 64) & (row < 67), row + 3, jnp.where((row >= 67) & (row < 70), row - 3, row))
    turn = (turn == col).astype(F32).astype(BF16)

    for level in range(1, LEVELS + 1):
        last = level - 1
        handed = accept(early[0], xch, last) + accept(early[1], xpk, last)
        arrive(handed[:1])
        own_f, other_f = och[last], xch[last]
        own_g = bdot(own_f, turn).astype(BF16)
        other_g = bdot(other_f, turn).astype(BF16)
        coupling = gauss(own_f, other_g)
        coupling_t = gauss(other_f, own_g)
        coup_out[last] = coupling
        store(coup_out.at[last], coup_hbm.at[0, last])
        onehot = onehots[last]
        fresh = bdot(onehot[:, :N], own_f) + bdot(onehot[:, N:], other_f)
        och[level] = dead_rows(fresh, 0, ranks_ref[0, level])
        arrive(handed[1:])
        arrive(accept(late, xcm, last))
        co[:N] = ocm[last]
        co[N:] = xcm[last]
        cy[:N] = opk[last] - dot3(coupling, xcm[last])
        cy[N:] = xpk[last] - dot3(coupling_t, ocm[last])
        cand = cy[...]
        picked = pick(onehot, cand)
        opk[level] = picked
        if level < LEVELS:
            early = swap(level)
        sum_step(level)
        factor = ridge_factor(picked)
        weight = dot6(dot6(picked, cand, NT), co[...])
        compressed = ridge_solve(factor, weight)
        if level < LEVELS:
            ocm[level] = compressed
            late = offer(ocm, xcm, level)
        else:
            top_out[...] = compressed
            store(top_out, top_hbm.at[0])
        interp = dot3(cand, ridge_solve(factor, picked), NT)
        at = is_upper[last] * N
        node_out[last, pl.ds(pl.multiple_of(at, N), N), :] = interp[:N]
        node_out[last, pl.ds(pl.multiple_of(N - at, N), N), :] = interp[N:]
        store(node_out.at[last], node_hbm.at[0, last])

    sum_step(4)
    store(tot.at[OWN], diag_hbm)
    for move in stores:
        move.wait()
    for copy in copies:
        copy.wait_send()


def finish(samples_ref, diag_ref, turn_ref, node_ref, coup_ref, top_ref, leaf_out, node_out, coup_out, top_out, sems):
    moves = [
        pltpu.make_async_copy(src, dst, sems.at[i])
        for i, (src, dst) in enumerate(((node_ref, node_out), (coup_ref, coup_out), (top_ref, top_out)))
    ]
    for move in moves:
        move.start()
    leaf_out[...] = dot3(samples_ref[...] - diag_ref[...], turn_ref[...], NT)
    for move in moves:
        move.wait()


N_COPIES = 14 * PIECES + 6 * (RING - 1) + 6 * (RING - 1) + 8 + 3 + 6 * (LEVELS - 1)


def shards(points, omega, samples, ranks, leaf_skeleton, merge_skeleton):
    vmem = pl.BlockSpec(memory_space=pltpu.VMEM)
    parts = pl.pallas_call(
        body,
        out_shape=(
            jax.ShapeDtypeStruct((N, N), F32),
            jax.ShapeDtypeStruct((N, N), F32),
            jax.ShapeDtypeStruct((1, LEVELS, 2 * N, N), F32),
            jax.ShapeDtypeStruct((1, LEVELS, N, N), F32),
            jax.ShapeDtypeStruct((1, N, N), F32),
        ),
        in_specs=[pl.BlockSpec(memory_space=pltpu.HBM)] * 6,
        out_specs=(pl.BlockSpec(memory_space=pltpu.HBM),) * 5,
        scratch_shapes=[
            pltpu.VMEM((RING, N, N + AUG), BF16),
            pltpu.VMEM((RING, N, N + AUG), BF16),
            pltpu.VMEM((RING, N, N), F32),
            pltpu.VMEM((2, 4, N, N), F32),
            pltpu.VMEM((N, AUG), BF16),
            pltpu.VMEM((RING, CUT, AUG), BF16),
            pltpu.VMEM((RING, CUT, AUG), BF16),
            pltpu.VMEM((CUT, AUG), BF16),
            pltpu.VMEM((LEVELS + 1, N, AUG), BF16),
            pltpu.VMEM((LEVELS, N, AUG), BF16),
            pltpu.VMEM((N, N), F32),
            pltpu.VMEM((RING, CUT, N), F32),
            pltpu.VMEM((RING, CUT, N), F32),
            pltpu.VMEM((LEVELS + 1, N, N), F32),
            pltpu.VMEM((LEVELS, N, N), F32),
            pltpu.VMEM((N, N), F32),
            pltpu.VMEM((2, RING, CUT // 2, N), F32),
            pltpu.VMEM((2, RING, CUT // 2, N), F32),
            pltpu.VMEM((N, N), F32),
            pltpu.VMEM((LEVELS, N, N), F32),
            pltpu.VMEM((LEVELS, N, N), F32),
            pltpu.VMEM((LEVELS, N, 2 * N), BF16),
            pltpu.VMEM((2 * N, N), F32),
            pltpu.VMEM((2 * N, N), F32),
            pltpu.VMEM(points.shape[::-1], BF16),
            pltpu.VMEM(omega.shape, BF16),
            pltpu.VMEM(leaf_skeleton.shape, jnp.int32),
            pltpu.SMEM(ranks.shape, jnp.int32),
            pltpu.VMEM(samples.shape, F32),
            pltpu.VMEM((LEVELS, 1, N), jnp.int32),
            pltpu.SemaphoreType.DMA((6,)),
            pltpu.VMEM((N, N), F32),
            pltpu.VMEM((LEVELS, 2 * N, N), F32),
            pltpu.VMEM((LEVELS, N, N), F32),
            pltpu.VMEM((N, N), F32),
            pltpu.SemaphoreType.DMA((2 * LEVELS + 3,)),
            pltpu.SemaphoreType.DMA((N_COPIES,)),
            pltpu.SemaphoreType.DMA((N_COPIES,)),
        ],
        compiler_params=pltpu.CompilerParams(
            collective_id=0, has_side_effects=True, vmem_limit_bytes=54 * 2**20
        ),
    )(omega, points.T, samples, leaf_skeleton, merge_skeleton.transpose(1, 0, 2), ranks)
    hold = pl.BlockSpec(memory_space=pl.ANY)
    return pl.pallas_call(
        finish,
        out_shape=(jax.ShapeDtypeStruct((N, N), F32),)
        + tuple(jax.ShapeDtypeStruct(part.shape, F32) for part in parts[2:]),
        in_specs=[vmem] * 3 + [hold] * 3,
        out_specs=(vmem,) + (hold,) * 3,
        scratch_shapes=[pltpu.SemaphoreType.DMA((3,))],
        compiler_params=pltpu.CompilerParams(vmem_limit_bytes=54 * 2**20),
    )(samples, *parts)


def solution(mesh):
    in_specs = (
        P(("leaf", "sub"), None),
        P(("leaf", "sub"), None),
        P(("leaf", "sub"), None),
        P("leaf", None),
        P("leaf", None),
        P("leaf", None, None),
    )
    out_specs = (
        P(("leaf", "sub"), None),
        P("leaf", None, None, None),
        P("leaf", None, None, None),
        P("leaf", None, None),
    )
    return jax.shard_map(shards, mesh=mesh, in_specs=in_specs, out_specs=out_specs, check_vma=False)
```

```python
import jax
import jax.numpy as jnp
from jax import lax
from jax.experimental import pallas as pl
from jax.experimental.pallas import tpu as pltpu
from jax.sharding import PartitionSpec as P

F32 = jnp.float32
BF16 = jnp.bfloat16
RING = 8
N = 256
AUG = 128
CUT = N // RING
PIECES = 4
LEVELS = 3
OWN = RING // 2 - 1
NN = ((1,), (0,))
NT = ((1,), (1,))
TN = ((0,), (0,))
DEAD = -1e30
MESH = pl.DeviceIdType.MESH

SPAN = N + 1.0
SIGMA = (SPAN + 1.0) / (SPAN - 1.0)
CHEB = 2.0 * SIGMA * SIGMA - 1.0
ALPHA = 8.0 * (SPAN + 1.0) / ((SPAN - 1.0) ** 2 * CHEB)
BETA = 8.0 / ((SPAN - 1.0) ** 2 * CHEB)
RATES = []
RHO = 1.0 / CHEB
for _ in range(6):
    RATES.append(2.0 / (2.0 - RHO * RHO))
    RHO = RHO * RHO / (2.0 - RHO * RHO)


def bdot(a, b, dims=NN):
    return lax.dot_general(a, b, (dims, ((), ())), preferred_element_type=F32)


def split2(x):
    hi = x.astype(BF16)
    return hi, (x - hi.astype(F32)).astype(BF16)


def split3(x):
    hi = x.astype(BF16)
    rest = x - hi.astype(F32)
    mid = rest.astype(BF16)
    return hi, mid, (rest - mid.astype(F32)).astype(BF16)


def dot3(a, b, dims=NN):
    ah, al = split2(a)
    bh, bl = split2(b)
    return bdot(ah, bh, dims) + (bdot(ah, bl, dims) + bdot(al, bh, dims))


def pick(onehot, x, dims=NN):
    hi, mid, lo = split3(x)
    return bdot(onehot, hi, dims) + bdot(onehot, mid, dims) + bdot(onehot, lo, dims)


def dot6(a, b, dims=NN):
    return lax.dot_general(
        a, b, (dims, ((), ())), precision=lax.Precision.HIGHEST, preferred_element_type=F32
    )


def iota(shape, dim):
    return lax.broadcasted_iota(jnp.int32, shape, dim)


def ridge_factor(p):
    gram = dot6(p, p, NT)
    inv_shift = 1.0 / (jnp.sum(p * p) / N + 1e-06)
    eye = (iota((N, N), 0) == iota((N, N), 1)).astype(F32)
    b = gram * inv_shift + eye
    x = ALPHA * eye - BETA * b
    e = eye - dot3(b, x)
    for step, w in enumerate(RATES):
        if step < 4:
            eh, el = split2(e)
            xh, xl = split2(x)
            e2 = bdot(eh, eh) + (bdot(eh, el) + bdot(el, eh))
            x = w * (x + (bdot(xh, eh) + (bdot(xh, el) + bdot(xl, eh))))
        else:
            eh = e.astype(BF16)
            e2 = bdot(eh, eh)
            x = w * (x + bdot(x.astype(BF16), eh))
        e = (1.0 - w) * eye + w * e2
    return b, x, inv_shift


def ridge_solve(factor, right):
    b, x, inv_shift = factor
    first = dot3(x, right)
    return (first + dot3(x, right - dot6(b, first))) * inv_shift


def gauss(left_f, right_g):
    return jnp.exp(bdot(left_f, right_g, NT) * 0.0625)


def body(
    omega_hbm, points_hbm, samples_hbm, skel_hbm, mskel_hbm, ranks_hbm,
    diag_hbm, turn_hbm, node_hbm, coup_hbm, top_hbm,
    zbuf, ybuf, tot, rsb,
    csp, crz, cry, cz, och, xch,
    psp, prz, pry, opk, xpk,
    kept, mtp, mr1, mr2, mfull, ocm, xcm, onehots, cy, co,
    points_ref, omega_ref, skel_ref, ranks_ref, samples_ref, mskel_ref, load_sem,
    turn_out, node_out, coup_out, top_out, store_sem, send_sem, recv_sem,
):
    loads = [
        pltpu.make_async_copy(src, dst, load_sem.at[i])
        for i, (src, dst) in enumerate((
            (points_hbm, points_ref), (omega_hbm, omega_ref), (skel_hbm, skel_ref),
            (ranks_hbm, ranks_ref), (samples_hbm, samples_ref), (mskel_hbm, mskel_ref),
        ))
    ]
    for load in loads:
        load.start()
    stores = []

    def store(src, dst):
        stores.append(pltpu.make_async_copy(src, dst, store_sem.at[len(stores)]))
        stores[-1].start()

    sub = lax.axis_index("sub")
    leaf = lax.axis_index("leaf")
    z = sub // RING
    y = sub % RING

    def zpeer(d):
        return {"sub": lax.rem(z + d + RING, RING) * RING + y}

    def ypeer(d):
        return {"sub": z * RING + lax.rem(y + d + RING, RING)}

    barrier = pltpu.get_barrier_semaphore()
    for d in range(1, RING):
        pl.semaphore_signal(barrier, inc=1, device_id=zpeer(d), device_id_type=MESH)
        pl.semaphore_signal(barrier, inc=1, device_id=ypeer(d), device_id_type=MESH)
    partners = []
    for level in range(LEVELS):
        bit = (leaf // 2**level) % 2
        partners.append({"leaf": leaf + (1 - 2 * bit) * 2**level})
        pl.semaphore_signal(barrier, inc=1, device_id=partners[-1], device_id_type=MESH)

    copies = []

    def send(src, dst, device):
        at = len(copies)
        copy = pltpu.make_async_remote_copy(
            src_ref=src, dst_ref=dst, send_sem=send_sem.at[at], recv_sem=recv_sem.at[at],
            device_id=device, device_id_type=MESH,
        )
        copy.start()
        copies.append(copy)
        return copy

    def arrive(group):
        for copy in group:
            copy.wait_recv()

    for load in loads[:4]:
        load.wait()

    eye = (iota((N, N), 0) == iota((N, N), 1)).astype(BF16)
    padded = jnp.concatenate([points_ref[...], jnp.zeros((AUG - 64, N), BF16)], axis=0)
    plain = bdot(eye, padded, NT)
    half = -0.5 * jnp.sum(plain * plain, axis=1, keepdims=True)
    h1, h2, h3 = (piece.astype(F32) for piece in split3(half))
    lane = iota((N, AUG), 1)

    def place(at, other):
        out = jnp.where((lane >= other) & (lane < other + 3), 1.0, plain)
        for i, piece in enumerate((h1, h2, h3)):
            out = jnp.where(lane == at + i, piece, out)
        return out.astype(BF16)

    feat = place(64, 67)
    omega = omega_ref[...]
    omega_t = bdot(eye, omega, NT).astype(BF16)
    zbuf[OWN, :, :N] = omega
    zbuf[OWN, :, N:] = place(67, 64)
    ybuf[OWN, :, :N] = omega_t
    ybuf[OWN, :, N:] = feat
    pl.semaphore_wait(barrier, 2 * (RING - 1) + LEVELS)

    def scatter(src, dst, peer, pos, rows):
        group = []
        for d in range(1, RING):
            to = lax.rem(pos + d, RING)
            group.append(
                send(src.at[pl.ds(pl.multiple_of(to * rows, rows), rows)], dst.at[d], peer(d))
            )
        return group

    def spread(dst, peer, pos):
        return [send(dst.at[pos], dst.at[pos], peer(d)) for d in range(1, RING)]

    def own_rows(pos, rows):
        return pl.ds(pl.multiple_of(pos * rows, rows), rows)

    def gather(full, peer, pos, rows, start=0):
        at = pl.ds(pl.multiple_of(start + pos * rows, rows), rows)
        return [send(full.at[at], full.at[at], peer(d)) for d in range(1, RING)]

    hr = N // 2
    top, bottom = pl.ds(0, hr), pl.ds(hr, hr)

    def right(axis, s, part):
        buf, peer = axis
        at = pl.ds(part * (N // PIECES), N // PIECES)
        return send(buf.at[OWN + s - 1, at], buf.at[OWN + s, at], peer(1))

    def left(axis, s, part):
        buf, peer = axis
        at = pl.ds(part * (N // PIECES), N // PIECES)
        to = OWN - s if s < 4 else OWN + 4
        return send(buf.at[OWN - s + 1, at], buf.at[to, at], peer(-1))

    axes = ((zbuf, zpeer), (ybuf, ypeer))
    ways = (right, left)
    flying = {}

    def launch(axis, way, s, part):
        if s < 4 or part * 2 // PIECES == way:
            flying[axis, way, s, part] = ways[way](axes[axis], s, part)

    for part in range(PIECES):
        for axis in range(2):
            for way in range(2):
                launch(axis, way, 1, part)

    column = iota((1, N), 1)
    offset = skel_ref[...] - sub * N
    hits = (iota((N, N), 0) == offset) & (column < ranks_ref[0, 0])
    hot = bdot(eye, hits.astype(F32).astype(BF16), NT).astype(BF16)
    csp[...] = bdot(hot, feat).astype(BF16)
    chosen_rs = scatter(csp, crz, zpeer, z, CUT)

    def block(r, c, first):
        weights = gauss(ybuf[r, :, N:], zbuf[c, :, N:]).astype(BF16)
        term = bdot(weights, zbuf[c, :, :N])
        if first:
            tot[r] = term
        else:
            tot[r] += term

    loads[5].wait()
    is_upper = [(leaf // 2**level) % 2 for level in range(LEVELS)]
    for level in range(LEVELS):
        index = mskel_ref[level]
        index = lax.rem(index + N * is_upper[level], 2 * N)
        wide = (iota((2 * N, N), 0) == index) & (column < ranks_ref[0, level + 1])
        onehots[level] = bdot(eye, wide.astype(F32).astype(BF16), NT).astype(BF16)

    def dead_rows(x, row0, rank):
        rows = x.shape[0]
        gone = iota((rows, AUG), 0) + row0 >= rank
        at = iota((rows, AUG), 1)
        x = jnp.where(gone & (at == 64), DEAD, x)
        return jnp.where(gone & (at == 67), 1.0, x).astype(BF16)

    def total_of(dst):
        total = dst[0].astype(F32)
        for d in range(1, RING):
            total += dst[d].astype(F32)
        return total

    seen = set()
    todo = [(OWN, OWN)]

    def work(pairs):
        for r, c in pairs:
            block(r, c, all((r, k) not in seen for k in range(RING)))
            seen.add((r, c))

    for s in range(1, 4):
        for part in range(PIECES):
            for axis in range(2):
                for way in range(2):
                    copy = flying.pop((axis, way, s, part), None)
                    if copy is not None:
                        copy.wait_recv()
                        launch(axis, way, s + 1, part)
            if s == 2 and part == PIECES - 1:
                loads[4].wait()
                psp[...] = pick(hot, samples_ref[...])
                picked_rs = scatter(psp, prz, zpeer, z, CUT)
            if s == 2 and part == 0:
                arrive(chosen_rs)
                total = csp[own_rows(z, CUT), :].astype(F32)
                for d in range(1, RING):
                    total += crz[d].astype(F32)
                cry[y] = total.astype(BF16)
                chosen_ag = spread(cry, ypeer, y)
            if s == 3 and part == PIECES - 1:
                arrive(chosen_ag)
                cz[...] = dead_rows(total_of(cry), z * CUT, ranks_ref[0, 0])
                och[0, own_rows(z, CUT), :] = cz[...]
                chosen_all = gather(och.at[0], zpeer, z, CUT)
            cut = len(todo) // (PIECES - part)
            work(todo[:cut])
            todo = todo[cut:]
        known = range(max(0, OWN - s), OWN + s + 1)
        todo = [(r, c) for c in known for r in known if (r, c) not in seen]

    work(todo)
    sh, sl = split2(samples_ref[...])
    mt = bdot(omega_t, sh) + bdot(omega_t, sl)
    far = RING - 1
    for r in range(far):
        th, tl = split2(tot[r])
        turned = ybuf[r, :, :N]
        mt -= bdot(turned, th) + bdot(turned, tl)
    mtp[...] = mt
    for copy in flying.values():
        copy.wait_recv()
    for c in range(far):
        block(far, c, c == 0)
    columns = jnp.zeros((N, N), F32)
    for r in range(RING):
        weights = gauss(ybuf[r, :, N:], zbuf[far, :, N:]).astype(BF16)
        kept[r] = weights
        columns += bdot(ybuf[r, :, :N], weights)
    th, tl = split2(tot[far])
    vh, vl = split2(columns)
    turned, plain_omega = ybuf[far, :, :N], zbuf[far, :, :N]
    mtp[...] -= bdot(turned, th) + bdot(turned, tl) + bdot(vh, plain_omega) + bdot(vl, plain_omega)
    halves = ((0, z, y, zpeer, ypeer), (hr, y, z, ypeer, zpeer))
    piece = hr // RING
    stage = []
    for i, (start, pos, other, first, second) in enumerate(halves):
        stage += scatter(mtp.at[pl.ds(start, hr)], mr1.at[i], first, pos, piece)

    arrive(picked_rs)
    total = psp[own_rows(z, CUT), :]
    for d in range(1, RING):
        total += prz[d]
    for c in range(RING):
        weights = gauss(cz[...], zbuf[c, :, N:]).astype(BF16)
        total -= bdot(weights, zbuf[c, :, :N])
    pry[y] = total
    picked_ag = spread(pry, ypeer, y)
    for r in range(RING):
        tot[r] += bdot(kept[r], zbuf[far, :, :N])

    flows = []

    def sum_step(s):
        if s > 0:
            arrive(flows[-1])
            if s == 1:
                tot[OWN - 3, :hr] += rsb[0, 0, :hr]
                tot[OWN + 3, hr:] += rsb[1, 0, hr:]
            else:
                tot[OWN - 4 + s] += rsb[0, s - 1]
                tot[OWN + 4 - s] += rsb[1, s - 1]
        if s == 0:
            flows.append([
                send(tot.at[OWN + 4, top], rsb.at[0, 0, top], ypeer(1)),
                send(tot.at[OWN + 4, bottom], rsb.at[1, 0, bottom], ypeer(-1)),
            ])
        elif s < 4:
            flows.append([
                send(tot.at[OWN - 4 + s], rsb.at[0, s], ypeer(1)),
                send(tot.at[OWN + 4 - s], rsb.at[1, s], ypeer(-1)),
            ])

    arrive(stage)
    stage = []
    for i, (start, pos, other, first, second) in enumerate(halves):
        at = pl.ds(pl.multiple_of(start + pos * piece, piece), piece)
        total = mtp[at, :]
        for d in range(1, RING):
            total += mr1[i, d]
        mr2[i, other] = total
        stage += spread(mr2.at[i], second, other)
    arrive(picked_ag)
    opk[0, own_rows(z, CUT), :] = total_of(pry)
    picked_all = gather(opk.at[0], zpeer, z, CUT)

    arrive(stage)
    stage = []
    for i, (start, pos, other, first, second) in enumerate(halves):
        at = pl.ds(pl.multiple_of(start + pos * piece, piece), piece)
        mfull[at, :] = total_of(mr2.at[i])
        stage += gather(mfull, first, pos, piece, start)

    arrive(chosen_all)
    arrive(picked_all)

    core = leaf % 2
    mate = partners[0]
    mine = pl.ds(pl.multiple_of(core * hr, hr), hr)

    def offer(src, dst, level):
        if level == 0:
            return [send(src.at[0], dst.at[0], mate)]
        return [send(src.at[level, mine], dst.at[level, mine], partners[level])]

    def accept(group, dst, level):
        arrive(group)
        if level > 0:
            return [send(dst.at[level, mine], dst.at[level, mine], mate)]
        return []

    def swap(level):
        return [offer(och, xch, level), offer(opk, xpk, level)]

    early = swap(0)
    sum_step(0)
    picked = opk[0]
    factor = ridge_factor(picked)
    arrive(stage)
    ocm[0] = ridge_solve(factor, dot6(picked, mfull[...], NT))
    late = offer(ocm, xcm, 0)
    leaf_factor = factor

    row = iota((AUG, AUG), 0)
    col = iota((AUG, AUG), 1)
    turn = jnp.where((row >= 64) & (row < 67), row + 3, jnp.where((row >= 67) & (row < 70), row - 3, row))
    turn = (turn == col).astype(F32).astype(BF16)

    for level in range(1, LEVELS + 1):
        last = level - 1
        handed = accept(early[0], xch, last) + accept(early[1], xpk, last)
        arrive(handed[:1])
        own_f, other_f = och[last], xch[last]
        own_g = bdot(own_f, turn).astype(BF16)
        other_g = bdot(other_f, turn).astype(BF16)
        coupling = gauss(own_f, other_g)
        coupling_t = gauss(other_f, own_g)
        coup_out[last] = coupling
        store(coup_out.at[last], coup_hbm.at[0, last])
        onehot = onehots[last]
        fresh = bdot(onehot[:, :N], own_f) + bdot(onehot[:, N:], other_f)
        och[level] = dead_rows(fresh, 0, ranks_ref[0, level])
        arrive(handed[1:])
        arrive(accept(late, xcm, last))
        co[:N] = ocm[last]
        co[N:] = xcm[last]
        cy[:N] = opk[last] - dot3(coupling, xcm[last])
        cy[N:] = xpk[last] - dot3(coupling_t, ocm[last])
        cand = cy[...]
        picked = pick(onehot, cand)
        opk[level] = picked
        if level < LEVELS:
            early = swap(level)
        sum_step(level)
        factor = ridge_factor(picked)
        weight = dot6(dot6(picked, cand, NT), co[...])
        if level < LEVELS:
            ocm[level] = ridge_solve(factor, weight)
            late = offer(ocm, xcm, level)
            turned = ridge_solve(factor, picked)
        else:
            both = ridge_solve(factor, jnp.concatenate([weight, picked], axis=1))
            top_out[...] = both[:, :N]
            store(top_out, top_hbm.at[0])
            turned = both[:, N:]
        if level == 1:
            turn_out[...] = ridge_solve(leaf_factor, opk[0])
            store(turn_out, turn_hbm)
        interp = dot3(cand, turned, NT)
        at = is_upper[last] * N
        node_out[last, pl.ds(pl.multiple_of(at, N), N), :] = interp[:N]
        node_out[last, pl.ds(pl.multiple_of(N - at, N), N), :] = interp[N:]
        store(node_out.at[last], node_hbm.at[0, last])

    sum_step(4)
    store(tot.at[OWN], diag_hbm)
    for move in stores:
        move.wait()
    for copy in copies:
        copy.wait_send()


def finish(
    samples_hbm, diag_hbm, turn_hbm, node_hbm, coup_hbm, top_hbm,
    leaf_out, node_out, coup_out, top_out,
    samples, diag, turn, leaf, node, coup, top, in_sem, out_sem,
):
    pairs = [(samples_hbm, samples), (diag_hbm, diag), (turn_hbm, turn)]
    moves = [(top_hbm.at[0], top, top_out.at[0])]
    for level in range(LEVELS):
        moves.append((coup_hbm.at[0, level], coup.at[level], coup_out.at[0, level]))
        moves.append((node_hbm.at[0, level], node.at[level], node_out.at[0, level]))
    pairs += [move[:2] for move in moves]
    loads = [pltpu.make_async_copy(*pair, in_sem.at[i]) for i, pair in enumerate(pairs)]
    for load in loads:
        load.start()
    stores = [pltpu.make_async_copy(*move[1:], out_sem.at[i]) for i, move in enumerate(moves)]
    for load in loads[:3]:
        load.wait()
    leaf[...] = dot3(samples[...] - diag[...], turn[...], NT)
    stores.append(pltpu.make_async_copy(leaf, leaf_out, out_sem.at[len(moves)]))
    stores[-1].start()
    for load, store in zip(loads[3:], stores):
        load.wait()
        store.start()
    for store in stores:
        store.wait()


N_COPIES = 14 * PIECES + 6 * (RING - 1) + 6 * (RING - 1) + 8 + 3 + 6 * (LEVELS - 1)


def shards(points, omega, samples, ranks, leaf_skeleton, merge_skeleton):
    parts = pl.pallas_call(
        body,
        out_shape=(
            jax.ShapeDtypeStruct((N, N), F32),
            jax.ShapeDtypeStruct((N, N), F32),
            jax.ShapeDtypeStruct((1, LEVELS, 2 * N, N), F32),
            jax.ShapeDtypeStruct((1, LEVELS, N, N), F32),
            jax.ShapeDtypeStruct((1, N, N), F32),
        ),
        in_specs=[pl.BlockSpec(memory_space=pltpu.HBM)] * 6,
        out_specs=(pl.BlockSpec(memory_space=pltpu.HBM),) * 5,
        scratch_shapes=[
            pltpu.VMEM((RING, N, N + AUG), BF16),
            pltpu.VMEM((RING, N, N + AUG), BF16),
            pltpu.VMEM((RING, N, N), F32),
            pltpu.VMEM((2, 4, N, N), F32),
            pltpu.VMEM((N, AUG), BF16),
            pltpu.VMEM((RING, CUT, AUG), BF16),
            pltpu.VMEM((RING, CUT, AUG), BF16),
            pltpu.VMEM((CUT, AUG), BF16),
            pltpu.VMEM((LEVELS + 1, N, AUG), BF16),
            pltpu.VMEM((LEVELS, N, AUG), BF16),
            pltpu.VMEM((N, N), F32),
            pltpu.VMEM((RING, CUT, N), F32),
            pltpu.VMEM((RING, CUT, N), F32),
            pltpu.VMEM((LEVELS + 1, N, N), F32),
            pltpu.VMEM((LEVELS, N, N), F32),
            pltpu.VMEM((RING, N, N), BF16),
            pltpu.VMEM((N, N), F32),
            pltpu.VMEM((2, RING, CUT // 2, N), F32),
            pltpu.VMEM((2, RING, CUT // 2, N), F32),
            pltpu.VMEM((N, N), F32),
            pltpu.VMEM((LEVELS, N, N), F32),
            pltpu.VMEM((LEVELS, N, N), F32),
            pltpu.VMEM((LEVELS, N, 2 * N), BF16),
            pltpu.VMEM((2 * N, N), F32),
            pltpu.VMEM((2 * N, N), F32),
            pltpu.VMEM(points.shape[::-1], BF16),
            pltpu.VMEM(omega.shape, BF16),
            pltpu.VMEM(leaf_skeleton.shape, jnp.int32),
            pltpu.SMEM(ranks.shape, jnp.int32),
            pltpu.VMEM(samples.shape, F32),
            pltpu.VMEM((LEVELS, 1, N), jnp.int32),
            pltpu.SemaphoreType.DMA((6,)),
            pltpu.VMEM((N, N), F32),
            pltpu.VMEM((LEVELS, 2 * N, N), F32),
            pltpu.VMEM((LEVELS, N, N), F32),
            pltpu.VMEM((N, N), F32),
            pltpu.SemaphoreType.DMA((2 * LEVELS + 3,)),
            pltpu.SemaphoreType.DMA((N_COPIES,)),
            pltpu.SemaphoreType.DMA((N_COPIES,)),
        ],
        compiler_params=pltpu.CompilerParams(
            collective_id=0, has_side_effects=True, vmem_limit_bytes=54 * 2**20
        ),
    )(omega, points.T, samples, leaf_skeleton, merge_skeleton.transpose(1, 0, 2), ranks)
    hold = pl.BlockSpec(memory_space=pl.ANY)
    return pl.pallas_call(
        finish,
        out_shape=(jax.ShapeDtypeStruct((N, N), F32),)
        + tuple(jax.ShapeDtypeStruct(part.shape, F32) for part in parts[2:]),
        in_specs=[hold] * 6,
        out_specs=(hold,) * 4,
        scratch_shapes=[pltpu.VMEM((N, N), F32)] * 4
        + [
            pltpu.VMEM((LEVELS, 2 * N, N), F32),
            pltpu.VMEM((LEVELS, N, N), F32),
            pltpu.VMEM((N, N), F32),
            pltpu.SemaphoreType.DMA((2 * LEVELS + 4,)),
            pltpu.SemaphoreType.DMA((2 * LEVELS + 2,)),
        ],
        compiler_params=pltpu.CompilerParams(vmem_limit_bytes=54 * 2**20),
    )(samples, *parts)


def solution(mesh):
    in_specs = (
        P(("leaf", "sub"), None),
        P(("leaf", "sub"), None),
        P(("leaf", "sub"), None),
        P("leaf", None),
        P("leaf", None),
        P("leaf", None, None),
    )
    out_specs = (
        P(("leaf", "sub"), None),
        P("leaf", None, None, None),
        P("leaf", None, None, None),
        P("leaf", None, None),
    )
    return jax.shard_map(shards, mesh=mesh, in_specs=in_specs, out_specs=out_specs, check_vma=False)
```

```python
import functools

import jax
import jax.numpy as jnp
from jax import lax
from jax.experimental import pallas as pl
from jax.experimental.pallas import tpu as pltpu
from jax.sharding import PartitionSpec as P

F32 = jnp.float32
BF16 = jnp.bfloat16
RING = 8
N = 256
AUG = 128
CUT = N // RING
PIECES = 4
LEVELS = 3
OWN = RING // 2 - 1
NN = ((1,), (0,))
NT = ((1,), (1,))
TN = ((0,), (0,))
DEAD = -1e30
MESH = pl.DeviceIdType.MESH

SPAN = N + 1.0
SIGMA = (SPAN + 1.0) / (SPAN - 1.0)
CHEB = 2.0 * SIGMA * SIGMA - 1.0
ALPHA = 8.0 * (SPAN + 1.0) / ((SPAN - 1.0) ** 2 * CHEB)
BETA = 8.0 / ((SPAN - 1.0) ** 2 * CHEB)
RATES = []
RHO = 1.0 / CHEB
for _ in range(6):
    RATES.append(2.0 / (2.0 - RHO * RHO))
    RHO = RHO * RHO / (2.0 - RHO * RHO)


def bdot(a, b, dims=NN):
    return lax.dot_general(a, b, (dims, ((), ())), preferred_element_type=F32)


def split2(x):
    hi = x.astype(BF16)
    return hi, (x - hi.astype(F32)).astype(BF16)


def split3(x):
    hi = x.astype(BF16)
    rest = x - hi.astype(F32)
    mid = rest.astype(BF16)
    return hi, mid, (rest - mid.astype(F32)).astype(BF16)


def dot3(a, b, dims=NN):
    ah, al = split2(a)
    bh, bl = split2(b)
    return bdot(ah, bh, dims) + (bdot(ah, bl, dims) + bdot(al, bh, dims))


def pick(onehot, x, dims=NN):
    hi, mid, lo = split3(x)
    return bdot(onehot, hi, dims) + bdot(onehot, mid, dims) + bdot(onehot, lo, dims)


def dot6(a, b, dims=NN):
    return lax.dot_general(
        a, b, (dims, ((), ())), precision=lax.Precision.HIGHEST, preferred_element_type=F32
    )


def iota(shape, dim):
    return lax.broadcasted_iota(jnp.int32, shape, dim)


def ridge_factor(p, beside=()):
    beside = list(beside)
    gram = dot6(p, p, NT)
    inv_shift = 1.0 / (jnp.sum(p * p) / N + 1e-06)
    eye = (iota((N, N), 0) == iota((N, N), 1)).astype(F32)
    b = gram * inv_shift + eye
    x = ALPHA * eye - BETA * b
    e = eye - dot3(b, x)
    for step, w in enumerate(RATES):
        if step < 4:
            eh, el = split2(e)
            xh, xl = split2(x)
            e2 = bdot(eh, eh) + (bdot(eh, el) + bdot(el, eh))
            x = w * (x + (bdot(xh, eh) + (bdot(xh, el) + bdot(xl, eh))))
        else:
            eh = e.astype(BF16)
            e2 = bdot(eh, eh)
            x = w * (x + bdot(x.astype(BF16), eh))
        e = (1.0 - w) * eye + w * e2
        if beside:
            beside.pop(0)()
    return b, x, inv_shift


def ridge_solve(factor, right):
    b, x, inv_shift = factor
    first = dot3(x, right)
    return (first + dot3(x, right - dot6(b, first))) * inv_shift


def gauss(left_f, right_g):
    return jnp.exp(bdot(left_f, right_g, NT) * 0.0625)


def body(
    omega_hbm, points_hbm, samples_hbm, skel_hbm, mskel_hbm, ranks_hbm,
    diag_hbm, turn_hbm, node_hbm, coup_hbm, top_hbm,
    zbuf, ybuf, tot, rsb,
    csp, crz, cry, cz, och, xch,
    psp, prz, pry, opk, xpk,
    kept, mtp, mr1, mr2, mfull, ocm, xcm, onehots, cy, co,
    points_ref, omega_ref, skel_ref, ranks_ref, samples_ref, mskel_ref, load_sem,
    turn_out, node_out, coup_out, top_out, store_sem, send_sem, recv_sem,
):
    loads = [
        pltpu.make_async_copy(src, dst, load_sem.at[i])
        for i, (src, dst) in enumerate((
            (points_hbm, points_ref), (omega_hbm, omega_ref), (skel_hbm, skel_ref),
            (ranks_hbm, ranks_ref), (samples_hbm, samples_ref), (mskel_hbm, mskel_ref),
        ))
    ]
    for load in loads:
        load.start()
    stores = []

    def store(src, dst):
        stores.append(pltpu.make_async_copy(src, dst, store_sem.at[len(stores)]))
        stores[-1].start()

    sub = lax.axis_index("sub")
    leaf = lax.axis_index("leaf")
    z = sub // RING
    y = sub % RING

    def zpeer(d):
        return {"sub": lax.rem(z + d + RING, RING) * RING + y}

    def ypeer(d):
        return {"sub": z * RING + lax.rem(y + d + RING, RING)}

    barrier = pltpu.get_barrier_semaphore()
    for d in range(1, RING):
        pl.semaphore_signal(barrier, inc=1, device_id=zpeer(d), device_id_type=MESH)
        pl.semaphore_signal(barrier, inc=1, device_id=ypeer(d), device_id_type=MESH)
    partners = []
    for level in range(LEVELS):
        bit = (leaf // 2**level) % 2
        partners.append({"leaf": leaf + (1 - 2 * bit) * 2**level})
        pl.semaphore_signal(barrier, inc=1, device_id=partners[-1], device_id_type=MESH)

    copies = []

    def send(src, dst, device):
        at = len(copies)
        copy = pltpu.make_async_remote_copy(
            src_ref=src, dst_ref=dst, send_sem=send_sem.at[at], recv_sem=recv_sem.at[at],
            device_id=device, device_id_type=MESH,
        )
        copy.start()
        copies.append(copy)
        return copy

    def arrive(group):
        for copy in group:
            copy.wait_recv()

    for load in loads[:4]:
        load.wait()

    eye = (iota((N, N), 0) == iota((N, N), 1)).astype(BF16)
    padded = jnp.concatenate([points_ref[...], jnp.zeros((AUG - 64, N), BF16)], axis=0)
    plain = bdot(eye, padded, NT)
    half = -0.5 * jnp.sum(plain * plain, axis=1, keepdims=True)
    h1, h2, h3 = (piece.astype(F32) for piece in split3(half))
    lane = iota((N, AUG), 1)

    def place(at, other):
        out = jnp.where((lane >= other) & (lane < other + 3), 1.0, plain)
        for i, piece in enumerate((h1, h2, h3)):
            out = jnp.where(lane == at + i, piece, out)
        return out.astype(BF16)

    feat = place(64, 67)
    omega = omega_ref[...]
    omega_t = bdot(eye, omega, NT).astype(BF16)
    zbuf[OWN, :, :N] = omega
    zbuf[OWN, :, N:] = place(67, 64)
    ybuf[OWN, :, :N] = omega_t
    ybuf[OWN, :, N:] = feat
    pl.semaphore_wait(barrier, 2 * (RING - 1) + LEVELS)

    def scatter(src, dst, peer, pos, rows):
        group = []
        for d in range(1, RING):
            to = lax.rem(pos + d, RING)
            group.append(
                send(src.at[pl.ds(pl.multiple_of(to * rows, rows), rows)], dst.at[d], peer(d))
            )
        return group

    def spread(dst, peer, pos):
        return [send(dst.at[pos], dst.at[pos], peer(d)) for d in range(1, RING)]

    def own_rows(pos, rows):
        return pl.ds(pl.multiple_of(pos * rows, rows), rows)

    def gather(full, peer, pos, rows, start=0):
        at = pl.ds(pl.multiple_of(start + pos * rows, rows), rows)
        return [send(full.at[at], full.at[at], peer(d)) for d in range(1, RING)]

    hr = N // 2
    top, bottom = pl.ds(0, hr), pl.ds(hr, hr)

    def right(axis, s, part):
        buf, peer = axis
        at = pl.ds(part * (N // PIECES), N // PIECES)
        return send(buf.at[OWN + s - 1, at], buf.at[OWN + s, at], peer(1))

    def left(axis, s, part):
        buf, peer = axis
        at = pl.ds(part * (N // PIECES), N // PIECES)
        to = OWN - s if s < 4 else OWN + 4
        return send(buf.at[OWN - s + 1, at], buf.at[to, at], peer(-1))

    axes = ((zbuf, zpeer), (ybuf, ypeer))
    ways = (right, left)
    flying = {}

    def launch(axis, way, s, part):
        if s < 4 or part * 2 // PIECES == way:
            flying[axis, way, s, part] = ways[way](axes[axis], s, part)

    for part in range(PIECES):
        for axis in range(2):
            for way in range(2):
                launch(axis, way, 1, part)

    column = iota((1, N), 1)
    offset = skel_ref[...] - sub * N
    hits = (iota((N, N), 0) == offset) & (column < ranks_ref[0, 0])
    hot = bdot(eye, hits.astype(F32).astype(BF16), NT).astype(BF16)
    csp[...] = bdot(hot, feat).astype(BF16)
    chosen_rs = scatter(csp, crz, zpeer, z, CUT)

    def block(r, c, first):
        weights = gauss(ybuf[r, :, N:], zbuf[c, :, N:]).astype(BF16)
        term = bdot(weights, zbuf[c, :, :N])
        if first:
            tot[r] = term
        else:
            tot[r] += term

    loads[5].wait()
    is_upper = [(leaf // 2**level) % 2 for level in range(LEVELS)]
    for level in range(LEVELS):
        index = mskel_ref[level]
        index = lax.rem(index + N * is_upper[level], 2 * N)
        wide = (iota((2 * N, N), 0) == index) & (column < ranks_ref[0, level + 1])
        onehots[level] = bdot(eye, wide.astype(F32).astype(BF16), NT).astype(BF16)

    def dead_rows(x, row0, rank):
        rows = x.shape[0]
        gone = iota((rows, AUG), 0) + row0 >= rank
        at = iota((rows, AUG), 1)
        x = jnp.where(gone & (at == 64), DEAD, x)
        return jnp.where(gone & (at == 67), 1.0, x).astype(BF16)

    def total_of(dst):
        total = dst[0].astype(F32)
        for d in range(1, RING):
            total += dst[d].astype(F32)
        return total

    seen = set()
    todo = [(OWN, OWN)]

    def work(pairs):
        for r, c in pairs:
            block(r, c, all((r, k) not in seen for k in range(RING)))
            seen.add((r, c))

    for s in range(1, 4):
        for part in range(PIECES):
            for axis in range(2):
                for way in range(2):
                    copy = flying.pop((axis, way, s, part), None)
                    if copy is not None:
                        copy.wait_recv()
                        launch(axis, way, s + 1, part)
            if s == 2 and part == PIECES - 1:
                loads[4].wait()
                psp[...] = pick(hot, samples_ref[...])
                picked_rs = scatter(psp, prz, zpeer, z, CUT)
            if s == 2 and part == 0:
                arrive(chosen_rs)
                total = csp[own_rows(z, CUT), :].astype(F32)
                for d in range(1, RING):
                    total += crz[d].astype(F32)
                cry[y] = total.astype(BF16)
                chosen_ag = spread(cry, ypeer, y)
            if s == 3 and part == PIECES - 1:
                arrive(chosen_ag)
                cz[...] = dead_rows(total_of(cry), z * CUT, ranks_ref[0, 0])
                och[0, own_rows(z, CUT), :] = cz[...]
                chosen_all = gather(och.at[0], zpeer, z, CUT)
            cut = len(todo) // (PIECES - part)
            work(todo[:cut])
            todo = todo[cut:]
        known = range(max(0, OWN - s), OWN + s + 1)
        todo = [(r, c) for c in known for r in known if (r, c) not in seen]

    work(todo)
    sh, sl = split2(samples_ref[...])
    mt = bdot(omega_t, sh) + bdot(omega_t, sl)
    far = RING - 1
    for r in range(far):
        th, tl = split2(tot[r])
        turned = ybuf[r, :, :N]
        mt -= bdot(turned, th) + bdot(turned, tl)
    mtp[...] = mt
    for copy in flying.values():
        copy.wait_recv()
    for c in range(far):
        block(far, c, c == 0)
    columns = jnp.zeros((N, N), F32)
    for r in range(RING):
        weights = gauss(ybuf[r, :, N:], zbuf[far, :, N:]).astype(BF16)
        kept[r] = weights
        columns += bdot(ybuf[r, :, :N], weights)
    th, tl = split2(tot[far])
    vh, vl = split2(columns)
    turned, plain_omega = ybuf[far, :, :N], zbuf[far, :, :N]
    mtp[...] -= bdot(turned, th) + bdot(turned, tl) + bdot(vh, plain_omega) + bdot(vl, plain_omega)
    halves = ((0, z, y, zpeer, ypeer), (hr, y, z, ypeer, zpeer))
    piece = hr // RING
    stage = []
    for i, (start, pos, other, first, second) in enumerate(halves):
        stage += scatter(mtp.at[pl.ds(start, hr)], mr1.at[i], first, pos, piece)

    arrive(picked_rs)
    total = psp[own_rows(z, CUT), :]
    for d in range(1, RING):
        total += prz[d]
    for c in range(RING):
        weights = gauss(cz[...], zbuf[c, :, N:]).astype(BF16)
        total -= bdot(weights, zbuf[c, :, :N])
    pry[y] = total
    picked_ag = spread(pry, ypeer, y)
    for r in range(RING):
        tot[r] += bdot(kept[r], zbuf[far, :, :N])

    flows = []

    def sum_step(s):
        if s > 0:
            arrive(flows[-1])
            if s == 1:
                tot[OWN - 3, :hr] += rsb[0, 0, :hr]
                tot[OWN + 3, hr:] += rsb[1, 0, hr:]
            else:
                tot[OWN - 4 + s] += rsb[0, s - 1]
                tot[OWN + 4 - s] += rsb[1, s - 1]
        if s == 0:
            flows.append([
                send(tot.at[OWN + 4, top], rsb.at[0, 0, top], ypeer(1)),
                send(tot.at[OWN + 4, bottom], rsb.at[1, 0, bottom], ypeer(-1)),
            ])
        elif s < 4:
            flows.append([
                send(tot.at[OWN - 4 + s], rsb.at[0, s], ypeer(1)),
                send(tot.at[OWN + 4 - s], rsb.at[1, s], ypeer(-1)),
            ])

    arrive(stage)
    stage = []
    for i, (start, pos, other, first, second) in enumerate(halves):
        at = pl.ds(pl.multiple_of(start + pos * piece, piece), piece)
        total = mtp[at, :]
        for d in range(1, RING):
            total += mr1[i, d]
        mr2[i, other] = total
        stage += spread(mr2.at[i], second, other)
    arrive(picked_ag)
    opk[0, own_rows(z, CUT), :] = total_of(pry)
    picked_all = gather(opk.at[0], zpeer, z, CUT)

    arrive(stage)
    stage = []
    for i, (start, pos, other, first, second) in enumerate(halves):
        at = pl.ds(pl.multiple_of(start + pos * piece, piece), piece)
        mfull[at, :] = total_of(mr2.at[i])
        stage += gather(mfull, first, pos, piece, start)

    arrive(chosen_all)
    arrive(picked_all)

    core = leaf % 2
    mate = partners[0]
    mine = pl.ds(pl.multiple_of(core * hr, hr), hr)

    def offer(src, dst, level):
        if level == 0:
            return [send(src.at[0], dst.at[0], mate)]
        return [send(src.at[level, mine], dst.at[level, mine], partners[level])]

    def accept(group, dst, level):
        arrive(group)
        if level > 0:
            return [send(dst.at[level, mine], dst.at[level, mine], mate)]
        return []

    def swap(level):
        return [offer(och, xch, level), offer(opk, xpk, level)]

    early = swap(0)
    sum_step(0)
    picked = opk[0]
    turned = ridge_solve(ridge_factor(picked), picked)
    turn_out[...] = turned
    store(turn_out, turn_hbm)
    arrive(stage)
    ocm[0] = dot6(turned, mfull[...], NT)
    late = offer(ocm, xcm, 0)
    sum_step(1)

    row = iota((AUG, AUG), 0)
    col = iota((AUG, AUG), 1)
    turn = jnp.where((row >= 64) & (row < 67), row + 3, jnp.where((row >= 67) & (row < 70), row - 3, row))
    turn = (turn == col).astype(F32).astype(BF16)

    for level in range(1, LEVELS + 1):
        last = level - 1
        handed = accept(early[0], xch, last) + accept(early[1], xpk, last)
        arrive(handed[:1])
        own_f, other_f = och[last], xch[last]
        own_g = bdot(own_f, turn).astype(BF16)
        other_g = bdot(other_f, turn).astype(BF16)
        coupling = gauss(own_f, other_g)
        coupling_t = gauss(other_f, own_g)
        coup_out[last] = coupling
        store(coup_out.at[last], coup_hbm.at[0, last])
        onehot = onehots[last]
        fresh = bdot(onehot[:, :N], own_f) + bdot(onehot[:, N:], other_f)
        och[level] = dead_rows(fresh, 0, ranks_ref[0, level])
        ch, cl = split2(coupling)
        co[:N] = ocm[last]
        arrive(handed[1:])
        cy[N:] = xpk[last] - dot3(coupling_t, ocm[last])
        from_other = pick(onehot[:, N:], cy[N:])
        arrive(accept(late, xcm, last))
        xh, xl = split2(xcm[last])
        own_new = opk[last] - (bdot(ch, xh) + (bdot(ch, xl) + bdot(cl, xh)))
        cy[:N] = own_new
        picked = pick(onehot[:, :N], own_new) + from_other
        co[N:] = xcm[last]
        cand = cy[...]
        opk[level] = picked
        if level < LEVELS:
            early = swap(level)
        made = {}

        def cross(name, rows):
            made[name] = dot6(made["p"], cy[rows], NT)

        def apply(name, rows):
            made[name] = dot6(made[name], co[rows])

        made["p"] = picked
        own_half, other_half = slice(0, N), slice(N, 2 * N)
        factor = ridge_factor(
            picked,
            [
                functools.partial(cross, "own", own_half),
                functools.partial(apply, "own", own_half),
                functools.partial(cross, "other", other_half),
                functools.partial(apply, "other", other_half),
            ],
        )
        weight = made["own"] + made["other"]
        if level < LEVELS:
            ocm[level] = ridge_solve(factor, weight)
            late = offer(ocm, xcm, level)
            turned = ridge_solve(factor, picked)
        else:
            both = ridge_solve(factor, jnp.concatenate([weight, picked], axis=1))
            top_out[...] = both[:, :N]
            store(top_out, top_hbm.at[0])
            turned = both[:, N:]
        interp = dot3(cand, turned, NT)
        at = is_upper[last] * N
        node_out[last, pl.ds(pl.multiple_of(at, N), N), :] = interp[:N]
        node_out[last, pl.ds(pl.multiple_of(N - at, N), N), :] = interp[N:]
        store(node_out.at[last], node_hbm.at[0, last])
        sum_step(level + 1)

    store(tot.at[OWN], diag_hbm)
    for move in stores:
        move.wait()
    for copy in copies:
        copy.wait_send()


def finish(
    samples_hbm, diag_hbm, turn_hbm, node_hbm, coup_hbm, top_hbm,
    leaf_out, node_out, coup_out, top_out,
    samples, diag, turn, leaf, node, coup, top, in_sem, out_sem,
):
    pairs = [(samples_hbm, samples), (diag_hbm, diag), (turn_hbm, turn)]
    moves = [(top_hbm.at[0], top, top_out.at[0])]
    for level in range(LEVELS):
        moves.append((coup_hbm.at[0, level], coup.at[level], coup_out.at[0, level]))
        moves.append((node_hbm.at[0, level], node.at[level], node_out.at[0, level]))
    pairs += [move[:2] for move in moves]
    loads = [pltpu.make_async_copy(*pair, in_sem.at[i]) for i, pair in enumerate(pairs)]
    for load in loads:
        load.start()
    stores = [pltpu.make_async_copy(*move[1:], out_sem.at[i]) for i, move in enumerate(moves)]
    for load in loads[:3]:
        load.wait()
    leaf[...] = dot3(samples[...] - diag[...], turn[...], NT)
    stores.append(pltpu.make_async_copy(leaf, leaf_out, out_sem.at[len(moves)]))
    stores[-1].start()
    for load, store in zip(loads[3:], stores):
        load.wait()
        store.start()
    for store in stores:
        store.wait()


N_COPIES = 14 * PIECES + 6 * (RING - 1) + 6 * (RING - 1) + 8 + 3 + 6 * (LEVELS - 1)


def shards(points, omega, samples, ranks, leaf_skeleton, merge_skeleton):
    parts = pl.pallas_call(
        body,
        out_shape=(
            jax.ShapeDtypeStruct((N, N), F32),
            jax.ShapeDtypeStruct((N, N), F32),
            jax.ShapeDtypeStruct((1, LEVELS, 2 * N, N), F32),
            jax.ShapeDtypeStruct((1, LEVELS, N, N), F32),
            jax.ShapeDtypeStruct((1, N, N), F32),
        ),
        in_specs=[pl.BlockSpec(memory_space=pltpu.HBM)] * 6,
        out_specs=(pl.BlockSpec(memory_space=pltpu.HBM),) * 5,
        scratch_shapes=[
            pltpu.VMEM((RING, N, N + AUG), BF16),
            pltpu.VMEM((RING, N, N + AUG), BF16),
            pltpu.VMEM((RING, N, N), F32),
            pltpu.VMEM((2, 4, N, N), F32),
            pltpu.VMEM((N, AUG), BF16),
            pltpu.VMEM((RING, CUT, AUG), BF16),
            pltpu.VMEM((RING, CUT, AUG), BF16),
            pltpu.VMEM((CUT, AUG), BF16),
            pltpu.VMEM((LEVELS + 1, N, AUG), BF16),
            pltpu.VMEM((LEVELS, N, AUG), BF16),
            pltpu.VMEM((N, N), F32),
            pltpu.VMEM((RING, CUT, N), F32),
            pltpu.VMEM((RING, CUT, N), F32),
            pltpu.VMEM((LEVELS + 1, N, N), F32),
            pltpu.VMEM((LEVELS, N, N), F32),
            pltpu.VMEM((RING, N, N), BF16),
            pltpu.VMEM((N, N), F32),
            pltpu.VMEM((2, RING, CUT // 2, N), F32),
            pltpu.VMEM((2, RING, CUT // 2, N), F32),
            pltpu.VMEM((N, N), F32),
            pltpu.VMEM((LEVELS, N, N), F32),
            pltpu.VMEM((LEVELS, N, N), F32),
            pltpu.VMEM((LEVELS, N, 2 * N), BF16),
            pltpu.VMEM((2 * N, N), F32),
            pltpu.VMEM((2 * N, N), F32),
            pltpu.VMEM(points.shape[::-1], BF16),
            pltpu.VMEM(omega.shape, BF16),
            pltpu.VMEM(leaf_skeleton.shape, jnp.int32),
            pltpu.SMEM(ranks.shape, jnp.int32),
            pltpu.VMEM(samples.shape, F32),
            pltpu.VMEM((LEVELS, 1, N), jnp.int32),
            pltpu.SemaphoreType.DMA((6,)),
            pltpu.VMEM((N, N), F32),
            pltpu.VMEM((LEVELS, 2 * N, N), F32),
            pltpu.VMEM((LEVELS, N, N), F32),
            pltpu.VMEM((N, N), F32),
            pltpu.SemaphoreType.DMA((2 * LEVELS + 3,)),
            pltpu.SemaphoreType.DMA((N_COPIES,)),
            pltpu.SemaphoreType.DMA((N_COPIES,)),
        ],
        compiler_params=pltpu.CompilerParams(
            collective_id=0, has_side_effects=True, vmem_limit_bytes=54 * 2**20
        ),
    )(omega, points.T, samples, leaf_skeleton, merge_skeleton.transpose(1, 0, 2), ranks)
    hold = pl.BlockSpec(memory_space=pl.ANY)
    return pl.pallas_call(
        finish,
        out_shape=(jax.ShapeDtypeStruct((N, N), F32),)
        + tuple(jax.ShapeDtypeStruct(part.shape, F32) for part in parts[2:]),
        in_specs=[hold] * 6,
        out_specs=(hold,) * 4,
        scratch_shapes=[pltpu.VMEM((N, N), F32)] * 4
        + [
            pltpu.VMEM((LEVELS, 2 * N, N), F32),
            pltpu.VMEM((LEVELS, N, N), F32),
            pltpu.VMEM((N, N), F32),
            pltpu.SemaphoreType.DMA((2 * LEVELS + 4,)),
            pltpu.SemaphoreType.DMA((2 * LEVELS + 2,)),
        ],
        compiler_params=pltpu.CompilerParams(vmem_limit_bytes=54 * 2**20),
    )(samples, *parts)


def solution(mesh):
    in_specs = (
        P(("leaf", "sub"), None),
        P(("leaf", "sub"), None),
        P(("leaf", "sub"), None),
        P("leaf", None),
        P("leaf", None),
        P("leaf", None, None),
    )
    out_specs = (
        P(("leaf", "sub"), None),
        P("leaf", None, None, None),
        P("leaf", None, None, None),
        P("leaf", None, None),
    )
    return jax.shard_map(shards, mesh=mesh, in_specs=in_specs, out_specs=out_specs, check_vma=False)
```

```python
import functools

import jax
import jax.numpy as jnp
from jax import lax
from jax.experimental import pallas as pl
from jax.experimental.pallas import tpu as pltpu
from jax.sharding import PartitionSpec as P

F32 = jnp.float32
BF16 = jnp.bfloat16
RING = 8
N = 256
AUG = 128
CUT = N // RING
PIECES = 4
LEVELS = 3
OWN = RING // 2 - 1
NN = ((1,), (0,))
NT = ((1,), (1,))
TN = ((0,), (0,))
DEAD = -1e30
MESH = pl.DeviceIdType.MESH

SPAN = N + 1.0
SIGMA = (SPAN + 1.0) / (SPAN - 1.0)
CHEB = 2.0 * SIGMA * SIGMA - 1.0
ALPHA = 8.0 * (SPAN + 1.0) / ((SPAN - 1.0) ** 2 * CHEB)
BETA = 8.0 / ((SPAN - 1.0) ** 2 * CHEB)
RATES = []
RHO = 1.0 / CHEB
for _ in range(6):
    RATES.append(2.0 / (2.0 - RHO * RHO))
    RHO = RHO * RHO / (2.0 - RHO * RHO)


def bdot(a, b, dims=NN):
    return lax.dot_general(a, b, (dims, ((), ())), preferred_element_type=F32)


def split2(x):
    hi = x.astype(BF16)
    return hi, (x - hi.astype(F32)).astype(BF16)


def split3(x):
    hi = x.astype(BF16)
    rest = x - hi.astype(F32)
    mid = rest.astype(BF16)
    return hi, mid, (rest - mid.astype(F32)).astype(BF16)


def dot3(a, b, dims=NN):
    ah, al = split2(a)
    bh, bl = split2(b)
    return bdot(ah, bh, dims) + (bdot(ah, bl, dims) + bdot(al, bh, dims))


def pick(onehot, x, dims=NN):
    hi, mid, lo = split3(x)
    return bdot(onehot, hi, dims) + bdot(onehot, mid, dims) + bdot(onehot, lo, dims)


def dot6(a, b, dims=NN):
    return lax.dot_general(
        a, b, (dims, ((), ())), precision=lax.Precision.HIGHEST, preferred_element_type=F32
    )


def iota(shape, dim):
    return lax.broadcasted_iota(jnp.int32, shape, dim)


def ridge_factor(p, beside=()):
    beside = list(beside)
    gram = dot6(p, p, NT)
    inv_shift = 1.0 / (jnp.sum(p * p) / N + 1e-06)
    eye = (iota((N, N), 0) == iota((N, N), 1)).astype(F32)
    b = gram * inv_shift + eye
    x = ALPHA * eye - BETA * b
    e = eye - dot3(b, x)
    for step, w in enumerate(RATES):
        if step < 3:
            eh, el = split2(e)
            xh, xl = split2(x)
            e2 = bdot(eh, eh) + (bdot(eh, el) + bdot(el, eh))
            x = w * (x + (bdot(xh, eh) + (bdot(xh, el) + bdot(xl, eh))))
        else:
            eh = e.astype(BF16)
            e2 = bdot(eh, eh)
            x = w * (x + bdot(x.astype(BF16), eh))
        e = (1.0 - w) * eye + w * e2
        if beside:
            beside.pop(0)()
    return b, x, inv_shift


def ridge_solve(factor, right):
    b, x, inv_shift = factor
    first = dot3(x, right)
    return (first + dot3(x, right - dot6(b, first))) * inv_shift


def gauss(left_f, right_g):
    return jnp.exp(bdot(left_f, right_g, NT) * 0.0625)


def body(
    omega_hbm, points_hbm, samples_hbm, skel_hbm, mskel_hbm, ranks_hbm,
    diag_hbm, turn_hbm, node_hbm, coup_hbm, top_hbm,
    zbuf, ybuf, tot, rsb,
    csp, crz, cry, cz, och, xch,
    psp, prz, pry, opk, xpk,
    kept, mtp, mr1, mr2, mfull, ocm, xcm, onehots, cy, co,
    points_ref, omega_ref, skel_ref, ranks_ref, samples_ref, mskel_ref, load_sem,
    turn_out, node_out, coup_out, top_out, store_sem, send_sem, recv_sem,
):
    loads = [
        pltpu.make_async_copy(src, dst, load_sem.at[i])
        for i, (src, dst) in enumerate((
            (points_hbm, points_ref), (omega_hbm, omega_ref), (skel_hbm, skel_ref),
            (ranks_hbm, ranks_ref), (samples_hbm, samples_ref), (mskel_hbm, mskel_ref),
        ))
    ]
    for load in loads:
        load.start()
    stores = []

    def store(src, dst):
        stores.append(pltpu.make_async_copy(src, dst, store_sem.at[len(stores)]))
        stores[-1].start()

    sub = lax.axis_index("sub")
    leaf = lax.axis_index("leaf")
    z = sub // RING
    y = sub % RING

    def zpeer(d):
        return {"sub": lax.rem(z + d + RING, RING) * RING + y}

    def ypeer(d):
        return {"sub": z * RING + lax.rem(y + d + RING, RING)}

    barrier = pltpu.get_barrier_semaphore()
    for d in range(1, RING):
        pl.semaphore_signal(barrier, inc=1, device_id=zpeer(d), device_id_type=MESH)
        pl.semaphore_signal(barrier, inc=1, device_id=ypeer(d), device_id_type=MESH)
    partners = []
    for level in range(LEVELS):
        bit = (leaf // 2**level) % 2
        partners.append({"leaf": leaf + (1 - 2 * bit) * 2**level})
        pl.semaphore_signal(barrier, inc=1, device_id=partners[-1], device_id_type=MESH)

    copies = []

    def send(src, dst, device):
        at = len(copies)
        copy = pltpu.make_async_remote_copy(
            src_ref=src, dst_ref=dst, send_sem=send_sem.at[at], recv_sem=recv_sem.at[at],
            device_id=device, device_id_type=MESH,
        )
        copy.start()
        copies.append(copy)
        return copy

    def arrive(group):
        for copy in group:
            copy.wait_recv()

    for load in loads[:4]:
        load.wait()

    eye = (iota((N, N), 0) == iota((N, N), 1)).astype(BF16)
    padded = jnp.concatenate([points_ref[...], jnp.zeros((AUG - 64, N), BF16)], axis=0)
    plain = bdot(eye, padded, NT)
    half = -0.5 * jnp.sum(plain * plain, axis=1, keepdims=True)
    h1, h2, h3 = (piece.astype(F32) for piece in split3(half))
    lane = iota((N, AUG), 1)

    def place(at, other):
        out = jnp.where((lane >= other) & (lane < other + 3), 1.0, plain)
        for i, piece in enumerate((h1, h2, h3)):
            out = jnp.where(lane == at + i, piece, out)
        return out.astype(BF16)

    feat = place(64, 67)
    omega = omega_ref[...]
    omega_t = bdot(eye, omega, NT).astype(BF16)
    zbuf[OWN, :, :N] = omega
    zbuf[OWN, :, N:] = place(67, 64)
    ybuf[OWN, :, :N] = omega_t
    ybuf[OWN, :, N:] = feat
    pl.semaphore_wait(barrier, 2 * (RING - 1) + LEVELS)

    def scatter(src, dst, peer, pos, rows):
        group = []
        for d in range(1, RING):
            to = lax.rem(pos + d, RING)
            group.append(
                send(src.at[pl.ds(pl.multiple_of(to * rows, rows), rows)], dst.at[d], peer(d))
            )
        return group

    def spread(dst, peer, pos):
        return [send(dst.at[pos], dst.at[pos], peer(d)) for d in range(1, RING)]

    def own_rows(pos, rows):
        return pl.ds(pl.multiple_of(pos * rows, rows), rows)

    def gather(full, peer, pos, rows, start=0):
        at = pl.ds(pl.multiple_of(start + pos * rows, rows), rows)
        return [send(full.at[at], full.at[at], peer(d)) for d in range(1, RING)]

    hr = N // 2
    top, bottom = pl.ds(0, hr), pl.ds(hr, hr)

    def right(axis, s, part):
        buf, peer = axis
        at = pl.ds(part * (N // PIECES), N // PIECES)
        return send(buf.at[OWN + s - 1, at], buf.at[OWN + s, at], peer(1))

    def left(axis, s, part):
        buf, peer = axis
        at = pl.ds(part * (N // PIECES), N // PIECES)
        to = OWN - s if s < 4 else OWN + 4
        return send(buf.at[OWN - s + 1, at], buf.at[to, at], peer(-1))

    axes = ((zbuf, zpeer), (ybuf, ypeer))
    ways = (right, left)
    flying = {}

    def launch(axis, way, s, part):
        if s < 4 or part * 2 // PIECES == way:
            flying[axis, way, s, part] = ways[way](axes[axis], s, part)

    for part in range(PIECES):
        for axis in range(2):
            for way in range(2):
                launch(axis, way, 1, part)

    column = iota((1, N), 1)
    offset = skel_ref[...] - sub * N
    hits = (iota((N, N), 0) == offset) & (column < ranks_ref[0, 0])
    hot = bdot(eye, hits.astype(F32).astype(BF16), NT).astype(BF16)
    csp[...] = bdot(hot, feat).astype(BF16)
    chosen_rs = scatter(csp, crz, zpeer, z, CUT)

    def block(r, c, first):
        weights = gauss(ybuf[r, :, N:], zbuf[c, :, N:]).astype(BF16)
        term = bdot(weights, zbuf[c, :, :N])
        if first:
            tot[r] = term
        else:
            tot[r] += term

    loads[5].wait()
    is_upper = [(leaf // 2**level) % 2 for level in range(LEVELS)]
    for level in range(LEVELS):
        index = mskel_ref[level]
        index = lax.rem(index + N * is_upper[level], 2 * N)
        wide = (iota((2 * N, N), 0) == index) & (column < ranks_ref[0, level + 1])
        onehots[level] = bdot(eye, wide.astype(F32).astype(BF16), NT).astype(BF16)

    def dead_rows(x, row0, rank):
        rows = x.shape[0]
        gone = iota((rows, AUG), 0) + row0 >= rank
        at = iota((rows, AUG), 1)
        x = jnp.where(gone & (at == 64), DEAD, x)
        return jnp.where(gone & (at == 67), 1.0, x).astype(BF16)

    def total_of(dst):
        total = dst[0].astype(F32)
        for d in range(1, RING):
            total += dst[d].astype(F32)
        return total

    seen = set()
    todo = [(OWN, OWN)]

    def work(pairs):
        for r, c in pairs:
            block(r, c, all((r, k) not in seen for k in range(RING)))
            seen.add((r, c))

    for s in range(1, 4):
        for part in range(PIECES):
            for axis in range(2):
                for way in range(2):
                    copy = flying.pop((axis, way, s, part), None)
                    if copy is not None:
                        copy.wait_recv()
                        launch(axis, way, s + 1, part)
            if s == 2 and part == PIECES - 1:
                loads[4].wait()
                psp[...] = pick(hot, samples_ref[...])
                picked_rs = scatter(psp, prz, zpeer, z, CUT)
            if s == 2 and part == 0:
                arrive(chosen_rs)
                total = csp[own_rows(z, CUT), :].astype(F32)
                for d in range(1, RING):
                    total += crz[d].astype(F32)
                cry[y] = total.astype(BF16)
                chosen_ag = spread(cry, ypeer, y)
            if s == 3 and part == PIECES - 1:
                arrive(chosen_ag)
                cz[...] = dead_rows(total_of(cry), z * CUT, ranks_ref[0, 0])
                och[0, own_rows(z, CUT), :] = cz[...]
                chosen_all = gather(och.at[0], zpeer, z, CUT)
            cut = len(todo) // (PIECES - part)
            work(todo[:cut])
            todo = todo[cut:]
        known = range(max(0, OWN - s), OWN + s + 1)
        todo = [(r, c) for c in known for r in known if (r, c) not in seen]

    work(todo)
    sh, sl = split2(samples_ref[...])
    mt = bdot(omega_t, sh) + bdot(omega_t, sl)
    far = RING - 1
    for r in range(far):
        th, tl = split2(tot[r])
        turned = ybuf[r, :, :N]
        mt -= bdot(turned, th) + bdot(turned, tl)
    mtp[...] = mt
    for copy in flying.values():
        copy.wait_recv()
    for c in range(far):
        block(far, c, c == 0)
    columns = jnp.zeros((N, N), F32)
    for r in range(RING):
        weights = gauss(ybuf[r, :, N:], zbuf[far, :, N:]).astype(BF16)
        kept[r] = weights
        columns += bdot(ybuf[r, :, :N], weights)
    th, tl = split2(tot[far])
    vh, vl = split2(columns)
    turned, plain_omega = ybuf[far, :, :N], zbuf[far, :, :N]
    mtp[...] -= bdot(turned, th) + bdot(turned, tl) + bdot(vh, plain_omega) + bdot(vl, plain_omega)
    halves = ((0, z, y, zpeer, ypeer), (hr, y, z, ypeer, zpeer))
    piece = hr // RING
    stage = []
    for i, (start, pos, other, first, second) in enumerate(halves):
        stage += scatter(mtp.at[pl.ds(start, hr)], mr1.at[i], first, pos, piece)

    arrive(picked_rs)
    total = psp[own_rows(z, CUT), :]
    for d in range(1, RING):
        total += prz[d]
    for c in range(RING):
        weights = gauss(cz[...], zbuf[c, :, N:]).astype(BF16)
        total -= bdot(weights, zbuf[c, :, :N])
    pry[y] = total
    picked_ag = spread(pry, ypeer, y)
    for r in range(RING):
        tot[r] += bdot(kept[r], zbuf[far, :, :N])

    flows = []

    def sum_step(s):
        if s > 0:
            arrive(flows[-1])
            if s == 1:
                tot[OWN - 3, :hr] += rsb[0, 0, :hr]
                tot[OWN + 3, hr:] += rsb[1, 0, hr:]
            else:
                tot[OWN - 4 + s] += rsb[0, s - 1]
                tot[OWN + 4 - s] += rsb[1, s - 1]
        if s == 0:
            flows.append([
                send(tot.at[OWN + 4, top], rsb.at[0, 0, top], ypeer(1)),
                send(tot.at[OWN + 4, bottom], rsb.at[1, 0, bottom], ypeer(-1)),
            ])
        elif s < 4:
            flows.append([
                send(tot.at[OWN - 4 + s], rsb.at[0, s], ypeer(1)),
                send(tot.at[OWN + 4 - s], rsb.at[1, s], ypeer(-1)),
            ])

    arrive(stage)
    stage = []
    for i, (start, pos, other, first, second) in enumerate(halves):
        at = pl.ds(pl.multiple_of(start + pos * piece, piece), piece)
        total = mtp[at, :]
        for d in range(1, RING):
            total += mr1[i, d]
        mr2[i, other] = total
        stage += spread(mr2.at[i], second, other)
    arrive(picked_ag)
    opk[0, own_rows(z, CUT), :] = total_of(pry)
    picked_all = gather(opk.at[0], zpeer, z, CUT)

    arrive(stage)
    stage = []
    for i, (start, pos, other, first, second) in enumerate(halves):
        at = pl.ds(pl.multiple_of(start + pos * piece, piece), piece)
        mfull[at, :] = total_of(mr2.at[i])
        stage += gather(mfull, first, pos, piece, start)

    arrive(chosen_all)
    arrive(picked_all)

    core = leaf % 2
    mate = partners[0]
    quarter = N // 4
    mine = [pl.ds(pl.multiple_of(core * hr + i * quarter, quarter), quarter) for i in range(2)]

    def offer(src, dst, level):
        if level == 0:
            return [send(src.at[0], dst.at[0], mate)]
        return [send(src.at[level, at], dst.at[level, at], partners[level]) for at in mine]

    def accept(group, dst, level):
        if level == 0:
            arrive(group)
            return []
        handed = []
        for copy, at in zip(group, mine):
            copy.wait_recv()
            handed.append(send(dst.at[level, at], dst.at[level, at], mate))
        return handed

    def swap(level):
        return [offer(och, xch, level), offer(opk, xpk, level)]

    early = swap(0)
    sum_step(0)
    picked = opk[0]
    turned = ridge_solve(ridge_factor(picked), picked)
    turn_out[...] = turned
    store(turn_out, turn_hbm)
    arrive(stage)
    ocm[0] = dot6(turned, mfull[...], NT)
    late = offer(ocm, xcm, 0)
    sum_step(1)

    row = iota((AUG, AUG), 0)
    col = iota((AUG, AUG), 1)
    turn = jnp.where((row >= 64) & (row < 67), row + 3, jnp.where((row >= 67) & (row < 70), row - 3, row))
    turn = (turn == col).astype(F32).astype(BF16)

    for level in range(1, LEVELS + 1):
        last = level - 1
        handed = accept(early[0], xch, last)
        handed_rows = accept(early[1], xpk, last)
        arrive(handed)
        own_f, other_f = och[last], xch[last]
        own_g = bdot(own_f, turn).astype(BF16)
        other_g = bdot(other_f, turn).astype(BF16)
        coupling = gauss(own_f, other_g)
        coupling_t = gauss(other_f, own_g)
        coup_out[last] = coupling
        store(coup_out.at[last], coup_hbm.at[0, last])
        onehot = onehots[last]
        fresh = bdot(onehot[:, :N], own_f) + bdot(onehot[:, N:], other_f)
        och[level] = dead_rows(fresh, 0, ranks_ref[0, level])
        ch, cl = split2(coupling)
        co[:N] = ocm[last]
        arrive(handed_rows)
        cy[N:] = xpk[last] - dot3(coupling_t, ocm[last])
        from_other = pick(onehot[:, N:], cy[N:])
        arrive(accept(late, xcm, last))
        xh, xl = split2(xcm[last])
        own_new = opk[last] - (bdot(ch, xh) + (bdot(ch, xl) + bdot(cl, xh)))
        cy[:N] = own_new
        picked = pick(onehot[:, :N], own_new) + from_other
        co[N:] = xcm[last]
        cand = cy[...]
        opk[level] = picked
        if level < LEVELS:
            early = swap(level)
        made = {}

        def cross(name, rows):
            made[name] = dot6(made["p"], cy[rows], NT)

        def apply(name, rows):
            made[name] = dot6(made[name], co[rows])

        made["p"] = picked
        own_half, other_half = slice(0, N), slice(N, 2 * N)
        factor = ridge_factor(
            picked,
            [
                functools.partial(cross, "own", own_half),
                functools.partial(apply, "own", own_half),
                functools.partial(cross, "other", other_half),
                functools.partial(apply, "other", other_half),
            ],
        )
        weight = made["own"] + made["other"]
        if level < LEVELS:
            ocm[level] = ridge_solve(factor, weight)
            late = offer(ocm, xcm, level)
            turned = ridge_solve(factor, picked)
        else:
            both = ridge_solve(factor, jnp.concatenate([weight, picked], axis=1))
            top_out[...] = both[:, :N]
            store(top_out, top_hbm.at[0])
            turned = both[:, N:]
        interp = dot3(cand, turned, NT)
        at = is_upper[last] * N
        node_out[last, pl.ds(pl.multiple_of(at, N), N), :] = interp[:N]
        node_out[last, pl.ds(pl.multiple_of(N - at, N), N), :] = interp[N:]
        store(node_out.at[last], node_hbm.at[0, last])
        sum_step(level + 1)

    store(tot.at[OWN], diag_hbm)
    for move in stores:
        move.wait()
    for copy in copies:
        copy.wait_send()


def finish(
    samples_hbm, diag_hbm, turn_hbm, node_hbm, coup_hbm, top_hbm,
    leaf_out, node_out, coup_out, top_out,
    samples, diag, turn, leaf, node, coup, top, in_sem, out_sem,
):
    pairs = [(samples_hbm, samples), (diag_hbm, diag), (turn_hbm, turn)]
    moves = [(top_hbm.at[0], top, top_out.at[0])]
    for level in range(LEVELS):
        moves.append((coup_hbm.at[0, level], coup.at[level], coup_out.at[0, level]))
        moves.append((node_hbm.at[0, level], node.at[level], node_out.at[0, level]))
    pairs += [move[:2] for move in moves]
    loads = [pltpu.make_async_copy(*pair, in_sem.at[i]) for i, pair in enumerate(pairs)]
    for load in loads:
        load.start()
    stores = [pltpu.make_async_copy(*move[1:], out_sem.at[i]) for i, move in enumerate(moves)]
    for load in loads[:3]:
        load.wait()
    leaf[...] = dot3(samples[...] - diag[...], turn[...], NT)
    stores.append(pltpu.make_async_copy(leaf, leaf_out, out_sem.at[len(moves)]))
    stores[-1].start()
    for load, store in zip(loads[3:], stores):
        load.wait()
        store.start()
    for store in stores:
        store.wait()


N_COPIES = 14 * PIECES + 6 * (RING - 1) + 6 * (RING - 1) + 8 + 3 + 12 * (LEVELS - 1)


def shards(points, omega, samples, ranks, leaf_skeleton, merge_skeleton):
    parts = pl.pallas_call(
        body,
        out_shape=(
            jax.ShapeDtypeStruct((N, N), F32),
            jax.ShapeDtypeStruct((N, N), F32),
            jax.ShapeDtypeStruct((1, LEVELS, 2 * N, N), F32),
            jax.ShapeDtypeStruct((1, LEVELS, N, N), F32),
            jax.ShapeDtypeStruct((1, N, N), F32),
        ),
        in_specs=[pl.BlockSpec(memory_space=pltpu.HBM)] * 6,
        out_specs=(pl.BlockSpec(memory_space=pltpu.HBM),) * 5,
        scratch_shapes=[
            pltpu.VMEM((RING, N, N + AUG), BF16),
            pltpu.VMEM((RING, N, N + AUG), BF16),
            pltpu.VMEM((RING, N, N), F32),
            pltpu.VMEM((2, 4, N, N), F32),
            pltpu.VMEM((N, AUG), BF16),
            pltpu.VMEM((RING, CUT, AUG), BF16),
            pltpu.VMEM((RING, CUT, AUG), BF16),
            pltpu.VMEM((CUT, AUG), BF16),
            pltpu.VMEM((LEVELS + 1, N, AUG), BF16),
            pltpu.VMEM((LEVELS, N, AUG), BF16),
            pltpu.VMEM((N, N), F32),
            pltpu.VMEM((RING, CUT, N), F32),
            pltpu.VMEM((RING, CUT, N), F32),
            pltpu.VMEM((LEVELS + 1, N, N), F32),
            pltpu.VMEM((LEVELS, N, N), F32),
            pltpu.VMEM((RING, N, N), BF16),
            pltpu.VMEM((N, N), F32),
            pltpu.VMEM((2, RING, CUT // 2, N), F32),
            pltpu.VMEM((2, RING, CUT // 2, N), F32),
            pltpu.VMEM((N, N), F32),
            pltpu.VMEM((LEVELS, N, N), F32),
            pltpu.VMEM((LEVELS, N, N), F32),
            pltpu.VMEM((LEVELS, N, 2 * N), BF16),
            pltpu.VMEM((2 * N, N), F32),
            pltpu.VMEM((2 * N, N), F32),
            pltpu.VMEM(points.shape[::-1], BF16),
            pltpu.VMEM(omega.shape, BF16),
            pltpu.VMEM(leaf_skeleton.shape, jnp.int32),
            pltpu.SMEM(ranks.shape, jnp.int32),
            pltpu.VMEM(samples.shape, F32),
            pltpu.VMEM((LEVELS, 1, N), jnp.int32),
            pltpu.SemaphoreType.DMA((6,)),
            pltpu.VMEM((N, N), F32),
            pltpu.VMEM((LEVELS, 2 * N, N), F32),
            pltpu.VMEM((LEVELS, N, N), F32),
            pltpu.VMEM((N, N), F32),
            pltpu.SemaphoreType.DMA((2 * LEVELS + 3,)),
            pltpu.SemaphoreType.DMA((N_COPIES,)),
            pltpu.SemaphoreType.DMA((N_COPIES,)),
        ],
        compiler_params=pltpu.CompilerParams(
            collective_id=0, has_side_effects=True, vmem_limit_bytes=54 * 2**20
        ),
    )(omega, points.T, samples, leaf_skeleton, merge_skeleton.transpose(1, 0, 2), ranks)
    hold = pl.BlockSpec(memory_space=pl.ANY)
    return pl.pallas_call(
        finish,
        out_shape=(jax.ShapeDtypeStruct((N, N), F32),)
        + tuple(jax.ShapeDtypeStruct(part.shape, F32) for part in parts[2:]),
        in_specs=[hold] * 6,
        out_specs=(hold,) * 4,
        scratch_shapes=[pltpu.VMEM((N, N), F32)] * 4
        + [
            pltpu.VMEM((LEVELS, 2 * N, N), F32),
            pltpu.VMEM((LEVELS, N, N), F32),
            pltpu.VMEM((N, N), F32),
            pltpu.SemaphoreType.DMA((2 * LEVELS + 4,)),
            pltpu.SemaphoreType.DMA((2 * LEVELS + 2,)),
        ],
        compiler_params=pltpu.CompilerParams(vmem_limit_bytes=54 * 2**20),
    )(samples, *parts)


def solution(mesh):
    in_specs = (
        P(("leaf", "sub"), None),
        P(("leaf", "sub"), None),
        P(("leaf", "sub"), None),
        P("leaf", None),
        P("leaf", None),
        P("leaf", None, None),
    )
    out_specs = (
        P(("leaf", "sub"), None),
        P("leaf", None, None, None),
        P("leaf", None, None, None),
        P("leaf", None, None),
    )
    return jax.shard_map(shards, mesh=mesh, in_specs=in_specs, out_specs=out_specs, check_vma=False)
```
